32 devices in a mesh: dp: 4 (over y, x), expert: 8 (over z, core).
Axes of the slice: x: 2, y: 2, z: 4, core: 2. Of those that a mesh axis runs over, the one named last changes fastest.
Arguments:
- routing: int32 [4096, 2], P(('dp', 'expert')), may hold values from 0 to 7, all different within a row; in each aligned block of 128 rows (0 to 127, 128 to 255, ...) at most 48 rows name the same one
- gates: float32 [4096, 2], P(('dp', 'expert')), may hold values from 0.1 to 1
- hidden: bfloat16 [4, 8, 8, 48, 768], P('dp', 'expert'), may hold values from -6 to 6
- w_down: bfloat16 [8, 768, 2048], P('expert'), may hold values from -0.21875 to 0.21875
- dout: bfloat16 [4096, 2048], P(('dp', 'expert')), may hold values from -6 to 6
Outputs:
- combined: bfloat16 [4096, 2048], P(('dp', 'expert'))
- grad_gates: float32 [4096, 2], P(('dp', 'expert'))
- grad_hidden: bfloat16 [4, 8, 8, 48, 768], P('dp', 'expert')
- grad_down: float32 [8, 768, 2048], P('expert', None, 'dp')
The draws below stay inside these ranges and needn't reach their ends.
Inputs may be any that keep to these rules, and one draw needn't show every extreme that they name: `routing`: in each aligned block of 128 rows (the rows of one device) no expert is named by more than 48 picks, and in some block an expert is named by exactly 48.
All inputs are finite; a program needn't handle non-finite values.
Results may differ from the reference program's by a relative error of at most 0.013.
Values may be sent and summed in bfloat16 or wider, within the bound.
No kernel may reach another device: no remote copies, remote signals or barrier semaphores. Data moves between devices by JAX's collectives and lax.ppermute only.
A program may use at most 64 MiB of HBM per device.

```python
import math
import jax
import jax.numpy as jnp
import numpy as np
from jax import lax

D = 2048
FF = 768
TOK_DEV = 128
TOP = 2
EXPERTS = 8
CAP = 48
TOKENS = 4096
N_DP = 4
N_EXPERT = 8


def raised(drawn, stream_key, source, target, shards_of, factor):
    def block_of(position):
        return (jnp.arange(drawn.shape[position]) // (drawn.shape[position] // shards_of)).reshape((-1,) + (1,) * (drawn.ndim - 1 - position))

    one_side = jax.random.permutation(stream_key, shards_of)[block_of(target)]
    other_side = (block_of(target) + shards_of // 2) % shards_of
    return jnp.where((block_of(source) == one_side) | (block_of(source) == other_side), factor * drawn, drawn)


def block_scale(key, dims, pieces, smallest, largest):
    def one(dim, blocks):
        draws = jax.random.uniform(jax.random.fold_in(jax.random.fold_in(key, 6), dim), (blocks,), jnp.float32, smallest / len(pieces), largest / len(pieces))
        return jnp.repeat(jnp.exp(draws), dims[dim] // blocks).reshape((-1,) + (1,) * (len(dims) - dim - 1))

    loudness = one(*pieces[0])
    for cut in pieces[1:]:
        loudness = loudness * one(*cut)
    return loudness


def routed_block(key, own, number, rows, number_of, top, reach, skew):
    sequence = jax.random.permutation(key, number_of)
    crowded, ordinary = shares(number_of, rows * top, reach, skew, True), shares(number_of, rows * top, reach, skew, False)
    places = jnp.arange(number_of)

    def named(lengths, offset_by):
        used = int((lengths > 0).sum())
        fixed = max(1, used // 4)
        shifted = fixed + (places - fixed + offset_by * (used - fixed)) % max(1, number_of - fixed)
        return jnp.zeros((number_of,), jnp.int32).at[sequence[jnp.where(places < fixed, places, shifted)]].set(jnp.asarray(lengths, jnp.int32))

    lengths = jnp.where(number % 4 == 0, named(crowded, number // 4), named(ordinary, number - number // 4 - 1))
    mixed = jax.random.permutation(jax.random.fold_in(own, 3), number_of)
    source_of, sink = mixed[0:number_of // 2 * 2:2], mixed[1:number_of // 2 * 2:2]
    slack = jnp.minimum(lengths[source_of] - 1, reach - lengths[sink]) // 2
    slack = jnp.where((source_of == sequence[0]) | (sink == sequence[0]) | (lengths[sink] == 0), 0, jnp.maximum(slack, 0))
    shifted = jax.random.randint(jax.random.fold_in(own, 4), (number_of // 2,), 0, 1 << 20) % (slack + 1)
    lengths = lengths.at[source_of].add(-shifted).at[sink].add(shifted)
    items = jnp.searchsorted(jnp.cumsum(lengths), jnp.arange(rows * top), side="right").astype(jnp.int32)
    grid = items.reshape(top, rows).T
    grid = grid[jax.random.permutation(jax.random.fold_in(own, 1), rows)]
    offset_by = jax.random.randint(jax.random.fold_in(own, 2), (rows, 1), 0, top)
    return jnp.take_along_axis(grid, (jnp.arange(top)[None, :] + offset_by) % top, axis=1)


def shares(count, total, reach, lean, full):
    loads = [(1 << 20) // math.isqrt(standing ** lean) + 1 for standing in range(1, count + 1)]
    largest = reach if full else min(reach, max(-(-total // count), total * loads[0] // sum(loads)))
    least = 1 if total - largest >= count - 1 else 0
    holding, surplus = [largest] + [least] * (count - 1), total - largest - least * (count - 1)
    while surplus > 0:
        candidates = [i for i in range(1, count) if holding[i] < largest] or [i for i in range(1, count) if holding[i] < reach]
        pool, left = sum([loads[i] for i in candidates]), surplus
        for i in candidates:
            more = min(reach - holding[i], max(1, left * loads[i] // pool), surplus)
            holding[i] = holding[i] + more
            surplus = surplus - more
    return np.array(holding)


def bell_draw(rng, shape, width, reach, cuts=(), kind=jnp.bfloat16):
    entries = width * jax.random.normal(rng, shape, jnp.float32)
    if cuts:
        entries = entries * block_scale(rng, shape, cuts, -0.22, 0.18)
    return jnp.clip(entries, -reach, reach).astype(kind)


def heavy_noise(key, dims, scale, bound, pieces, heavy, held_as=jnp.bfloat16):
    drawn = scale * jax.random.normal(key, dims, jnp.float32)
    if pieces:
        drawn = drawn * block_scale(key, dims, pieces, -0.22, 0.18)
    return jnp.clip(raised(drawn, jax.random.fold_in(key, 3), *heavy), -bound, bound).astype(held_as)


def setup_inputs(seed: int = 0) -> dict:
    streams_of = jax.random.split(jax.random.key(seed), 6)
    routing_keys = jax.random.split(jax.random.fold_in(streams_of[0], 1), TOKENS // TOK_DEV)
    routing_turns = jax.random.permutation(jax.random.fold_in(streams_of[0], 3), TOKENS // TOK_DEV)
    routing = jax.vmap(lambda own, number: routed_block(jax.random.fold_in(streams_of[0], 2), own, number, TOK_DEV, EXPERTS, TOP, CAP, 2))(routing_keys, routing_turns).reshape((TOKENS, TOP))
    gates = jnp.clip(jnp.exp(math.log(1.0) - 2.3025851 * jax.random.uniform(streams_of[1], (TOKENS, TOP), jnp.float32) ** block_scale(streams_of[1], (TOKENS, TOP), ((0, 32),), -0.2, 0.2)), 0.1, 1.0)
    hidden = bell_draw(streams_of[2], (N_DP, EXPERTS, N_EXPERT, CAP, FF), 1.0, 6.0, ((0, 4), (1, 8)))
    w_down = bell_draw(streams_of[3], (EXPERTS, FF, D), FF ** -0.5, 0.21875, ((0, 8),))
    dout = heavy_noise(streams_of[4], (TOKENS, D), 1.0, 6.0, ((0, 32),), (0, 1, 32, 2.75))
    return dict(routing=routing, gates=gates, hidden=hidden, w_down=w_down, dout=dout)


def ranks_of(picks_block):
    onehot = (picks_block[:, None] == jnp.arange(EXPERTS, dtype=jnp.int32)[None, :]).astype(jnp.int32)
    before = jnp.cumsum(onehot, axis=0) - onehot
    return jnp.sum(before * onehot, axis=1).astype(jnp.int32)


def reference(routing, gates, hidden, w_down, dout):
    chosen_all = routing.reshape(N_DP, N_EXPERT, TOK_DEV * TOP)
    rankings = jax.vmap(jax.vmap(ranks_of))(chosen_all)
    gate_split = gates.reshape(N_DP, N_EXPERT, TOK_DEV, TOP)
    grad_split = dout.reshape(N_DP, N_EXPERT, TOK_DEV, D)
    weight_float = w_down.astype(jnp.float32)
    sources = jnp.arange(N_EXPERT, dtype=jnp.int32)[:, None]

    def per_group_step(total, item):
        hidden_block, chosen, ranking, gate_block, grad_block = item
        expert_out = jnp.einsum("esrf,efd->esrd", hidden_block.astype(jnp.float32), weight_float).astype(jnp.bfloat16)
        picked = expert_out[chosen, sources, ranking].reshape(N_EXPERT, TOK_DEV, TOP, D).astype(jnp.float32)
        mixture = jnp.sum(gate_block[..., None] * picked, axis=2).astype(jnp.bfloat16)
        grad_float = grad_block.astype(jnp.float32)
        gate_grads = jnp.sum(picked * grad_float[:, :, None, :], axis=3)
        scaled = (gate_block[..., None] * grad_float[:, :, None, :]).astype(jnp.bfloat16).reshape(N_EXPERT, TOK_DEV * TOP, D)
        slot_grads = jnp.zeros((EXPERTS, N_EXPERT, CAP, D), jnp.bfloat16).at[chosen, sources, ranking].set(scaled)
        hidden_grads = jnp.einsum("esrd,efd->esrf", slot_grads.astype(jnp.float32), weight_float).astype(jnp.bfloat16)
        partial_value = jnp.einsum("esrf,esrd->efd", hidden_block.astype(jnp.float32), slot_grads.astype(jnp.float32)).astype(jnp.bfloat16)
        return total + partial_value.astype(jnp.float32), (mixture, gate_grads, hidden_grads)

    start = jnp.zeros((EXPERTS, FF, D), jnp.float32)
    total, (mixture, gate_grads, hidden_grads) = lax.scan(per_group_step, start, (hidden, chosen_all, rankings, gate_split, grad_split))
    return mixture.reshape(TOKENS, D), gate_grads.reshape(TOKENS, TOP), hidden_grads, total
```

```python
import functools

import jax
import jax.numpy as jnp
from jax import lax
from jax.experimental import pallas as pl
from jax.experimental.pallas import tpu as pltpu
from jax.sharding import PartitionSpec as P

WIDEST = 8
MIB = 1 << 20


def call(body, out_shape, args, flops=0, scratch=(), vmem=40):
    moved = sum(a.size * a.dtype.itemsize for a in jax.tree.leaves((args, out_shape)))
    return pl.pallas_call(
        body,
        out_shape=out_shape,
        scratch_shapes=scratch,
        compiler_params=pltpu.CompilerParams(vmem_limit_bytes=vmem * MIB),
        cost_estimate=pl.CostEstimate(flops=flops, bytes_accessed=moved, transcendentals=0),
    )(*args)


def as_row(column):
    rows = column.shape[0]
    diagonal = lax.broadcasted_iota(jnp.int32, (rows, rows), 0) == lax.broadcasted_iota(
        jnp.int32, (rows, rows), 1
    )
    return jnp.sum(jnp.where(diagonal, column, 0.0), axis=0, keepdims=True)


def slot_columns(named, experts, capacity):
    tokens, picks = named.shape
    lane = lax.broadcasted_iota(jnp.int32, (tokens, experts), 1)
    onehots = [(named[:, k : k + 1] == lane).astype(jnp.float32) for k in range(picks)]
    counted = functools.reduce(jnp.add, onehots)
    earlier = lax.broadcasted_iota(jnp.int32, (tokens, tokens), 0) > lax.broadcasted_iota(
        jnp.int32, (tokens, tokens), 1
    )
    before = jnp.dot(
        earlier.astype(jnp.bfloat16),
        counted.astype(jnp.bfloat16),
        preferred_element_type=jnp.float32,
    )
    return [
        named[:, k : k + 1].astype(jnp.float32) * capacity
        + jnp.sum(before * onehots[k], axis=1, keepdims=True)
        for k in range(picks)
    ]


def spread_body(experts, capacity, routing_ref, gates_ref, dout_ref, *block_refs):
    me = lax.axis_index("expert")
    tokens, picks = routing_ref.shape
    slots = slot_columns(routing_ref[...] ^ me, experts, capacity)
    gates = gates_ref[...]
    slot_rows = [as_row(s) for s in slots]
    gate_rows = [as_row(gates[:, k : k + 1]) for k in range(picks)]
    for m, block in enumerate(block_refs):
        here = lax.broadcasted_iota(jnp.int32, (capacity, tokens), 0).astype(jnp.float32) + m * capacity
        hits = [here == row for row in slot_rows]
        chosen = functools.reduce(jnp.logical_or, hits).astype(jnp.bfloat16)
        gate = functools.reduce(
            jnp.add,
            [jnp.sum(jnp.where(h, g, 0.0), axis=1, keepdims=True) for h, g in zip(hits, gate_rows)],
        )
        rows = jnp.dot(chosen, dout_ref[...], preferred_element_type=jnp.float32)
        block[...] = (rows * gate).astype(jnp.bfloat16)


def expert_body(hidden_ref, weight_ref, *block_refs):
    me = lax.axis_index("expert")
    capacity = hidden_ref.shape[1]
    rows = jnp.concatenate([hidden_ref[me ^ m] for m in range(len(block_refs))], axis=0)
    out = jnp.dot(rows, weight_ref[...], preferred_element_type=jnp.float32).astype(jnp.bfloat16)
    for m, block in enumerate(block_refs):
        block[...] = out[m * capacity : (m + 1) * capacity]


def hidden_grad_body(groups, *refs):
    *block_refs, weight_ref, grad_ref = refs[: -groups]
    slice_refs = refs[-groups:]
    me = lax.axis_index("expert")
    group = lax.axis_index("dp")
    capacity = block_refs[0].shape[0]
    rows = jnp.concatenate([b[...] for b in block_refs], axis=0)
    grad = lax.dot_general(
        rows, weight_ref[...], (((1,), (1,)), ((), ())), preferred_element_type=jnp.float32
    ).astype(jnp.bfloat16)
    for m in range(len(block_refs)):
        grad_ref[me ^ m] = grad[m * capacity : (m + 1) * capacity]
    width = slice_refs[0].shape[1]
    for d, part in enumerate(slice_refs):
        columns = pl.ds(pl.multiple_of((group ^ d) * width, width), width)
        for m, b in enumerate(block_refs):
            part[m * capacity : (m + 1) * capacity] = b[:, columns]


def weight_grad_body(groups, *refs):
    hidden_refs, slice_refs, out_ref = refs[:groups], refs[groups : 2 * groups], refs[-1]
    me = lax.axis_index("expert")
    experts = hidden_refs[0].shape[0]
    total = jnp.zeros(out_ref.shape, jnp.float32)
    for h, s in zip(hidden_refs, slice_refs):
        rows = jnp.concatenate([h[me ^ m] for m in range(experts)], axis=0)
        total += lax.dot_general(
            rows, s[...], (((0,), (0,)), ((), ())), preferred_element_type=jnp.float32
        )
    out_ref[...] = total


def combine_body(experts, capacity, routing_ref, gates_ref, dout_ref, *refs):
    block_refs, combined_ref, grad_gates_ref = refs[:-2], refs[-2], refs[-1]
    me = lax.axis_index("expert")
    tokens, picks = routing_ref.shape
    slots = slot_columns(routing_ref[...] ^ me, experts, capacity)
    gates = gates_ref[...]
    lane = lax.broadcasted_iota(jnp.int32, (tokens, experts * capacity), 1).astype(jnp.float32)
    rows = jnp.concatenate([b[...] for b in block_refs], axis=0)
    dout = dout_ref[...].astype(jnp.float32)
    total = 0.0
    for k in range(picks):
        chosen = (lane == slots[k]).astype(jnp.bfloat16)
        picked = jnp.dot(chosen, rows, preferred_element_type=jnp.float32)
        total += gates[:, k : k + 1] * picked
        grad_gates_ref[:, k : k + 1] = jnp.sum(picked * dout, axis=1, keepdims=True)
    combined_ref[...] = total.astype(jnp.bfloat16)


def pairs(size, m):
    return [(i, i ^ m) for i in range(size)]


def exchange(blocks, axis):
    size = lax.axis_size(axis)
    got = {0: blocks[0]}
    for m in reversed(range(1, size)):
        got[m] = lax.ppermute(blocks[m], axis, pairs(size, m))
    return [got[m] for m in range(size)]


def on_device(routing, gates, hidden, w_down, dout):
    experts = lax.axis_size("expert")
    groups = lax.axis_size("dp")
    capacity, units = hidden.shape[3:]
    width = w_down.shape[2]
    tokens, picks = routing.shape
    own = hidden[0, 0]
    weight = w_down[0]
    flops = 2 * experts * capacity * units * width
    block = jax.ShapeDtypeStruct((capacity, width), jnp.bfloat16)

    sent = call(
        functools.partial(spread_body, experts, capacity), [block] * experts, (routing, gates, dout),
        flops=2 * experts * capacity * tokens * width,
    )
    arrived = exchange(sent, "expert")
    outputs = call(expert_body, [block] * experts, (own, weight), flops=flops)
    returned = exchange(outputs, "expert")
    peers = exchange([own] * groups, "dp")
    grad_hidden, *slices = call(
        functools.partial(hidden_grad_body, groups),
        [jax.ShapeDtypeStruct(own.shape, jnp.bfloat16)]
        + [jax.ShapeDtypeStruct((experts * capacity, width // groups), jnp.bfloat16)] * groups,
        (*arrived, weight),
        flops=flops,
    )
    gathered = exchange(slices, "dp")
    grad_down = call(
        functools.partial(weight_grad_body, groups),
        jax.ShapeDtypeStruct((units, width // groups), jnp.float32),
        (*peers, *gathered),
        flops=flops,
    )
    combined, grad_gates = call(
        functools.partial(combine_body, experts, capacity),
        [
            jax.ShapeDtypeStruct((tokens, width), jnp.bfloat16),
            jax.ShapeDtypeStruct((tokens, picks), jnp.float32),
        ],
        (routing, gates, dout, *returned),
        flops=2 * picks * experts * capacity * tokens * width,
    )
    return (combined, grad_gates, grad_hidden[None, None], grad_down[None])


def slot_index(routing, experts, capacity):
    flattened = routing.reshape(-1)
    onehot = (flattened[:, None] == jnp.arange(experts, dtype=jnp.int32)[None, :]).astype(jnp.int32)
    before = jnp.cumsum(onehot, axis=0) - onehot
    ranking = jnp.sum(before * onehot, axis=1)
    return flattened * capacity + ranking


def on_device_wide(routing, gates, hidden, w_down, dout):
    experts = lax.axis_size("expert")
    capacity = hidden.shape[3]
    hidden_units = w_down.shape[1]
    model_width = w_down.shape[2]
    tok_rows = routing.shape[0]
    picks_per = routing.shape[1]
    weight = w_down[0]
    input_rows = hidden[0, 0].reshape(-1, hidden_units)
    outputs = jnp.dot(input_rows, weight, preferred_element_type=jnp.float32).astype(jnp.bfloat16)
    outputs = outputs.reshape(experts, capacity, model_width)
    returned = lax.all_to_all(outputs, "expert", split_axis=0, concat_axis=0, tiled=True)
    location = slot_index(routing, experts, capacity)
    picked = jnp.take(returned.reshape(experts * capacity, model_width), location, axis=0)
    picked = picked.reshape(tok_rows, picks_per, model_width).astype(jnp.float32)
    combined = jnp.sum(gates[..., None] * picked, axis=1).astype(jnp.bfloat16)
    grad_float = dout.astype(jnp.float32)
    grad_gates = jnp.sum(picked * grad_float[:, None, :], axis=2)
    scaled = (
        (gates[..., None] * grad_float[:, None, :]).astype(jnp.bfloat16).reshape(-1, model_width)
    )
    slot_grads = jnp.zeros((experts * capacity, model_width), jnp.bfloat16).at[location].set(scaled)
    slot_grads = slot_grads.reshape(experts, capacity, model_width)
    received = lax.all_to_all(slot_grads, "expert", split_axis=0, concat_axis=0, tiled=True)
    flattened = received.reshape(-1, model_width)
    grad_rows = lax.dot_general(
        flattened, weight, (((1,), (1,)), ((), ())), preferred_element_type=jnp.float32
    )
    grad_hidden = grad_rows.astype(jnp.bfloat16).reshape(experts, capacity, hidden_units)
    partial_grad = lax.dot_general(
        input_rows, flattened, (((0,), (0,)), ((), ())), preferred_element_type=jnp.float32
    )
    grad_down = lax.psum_scatter(
        partial_grad.astype(jnp.bfloat16), "dp", scatter_dimension=1, tiled=True
    ).astype(jnp.float32)
    return (combined, grad_gates, grad_hidden[None, None], grad_down[None])


def solution(mesh):
    placed = (
        P(("dp", "expert"), None),
        P(("dp", "expert"), None),
        P("dp", "expert", None, None, None),
        P("expert", None, None),
        P(("dp", "expert"), None),
    )
    pairwise = all(size <= WIDEST and size & (size - 1) == 0 for size in mesh.shape.values())
    return jax.shard_map(
        on_device if pairwise else on_device_wide,
        mesh=mesh,
        in_specs=placed,
        out_specs=(
            P(("dp", "expert"), None),
            P(("dp", "expert"), None),
            P("dp", "expert", None, None, None),
            P("expert", None, "dp"),
        ),
        check_vma=False,
    )
```

```python
import functools

import jax
import jax.numpy as jnp
from jax import lax
from jax.experimental import pallas as pl
from jax.experimental.pallas import tpu as pltpu
from jax.sharding import PartitionSpec as P

LINE = 8
SQUARE = 4
LANES = 128
PIECES = 3
MIB = 1 << 20
VMEM_ALL = 60
f32, bf16 = jnp.float32, jnp.bfloat16


class Steps:
    def __init__(self):
        self.token = None

    def __call__(self, body, outs, args, scratch=(), vmem=40, aliases=None, anywhere=(), anywhere_out=(), pinned=()):
        aliases = aliases or {}
        whole = pl.BlockSpec(memory_space=pltpu.VMEM)
        free = pl.BlockSpec(memory_space=pl.ANY)
        fixed = pl.BlockSpec(memory_space=pltpu.HBM)
        in_specs = [
            fixed if i in pinned else free if i in aliases or i in anywhere else whole
            for i in range(len(args))
        ]
        out_specs = [free if o in aliases.values() or o in anywhere_out else whole for o in range(len(outs))]
        n_args, n_outs = len(args), len(outs)
        chained = () if self.token is None else (self.token,)

        def kernel(*refs):
            rest = refs[n_args + len(chained) :]
            body(*refs[:n_args], *rest[:n_outs], *rest[n_outs + 1 :])

        *results, self.token = pl.pallas_call(
            kernel,
            out_shape=[*outs, jax.ShapeDtypeStruct((8, LANES), f32)],
            in_specs=in_specs + [free] * len(chained),
            out_specs=out_specs + [free],
            scratch_shapes=scratch,
            input_output_aliases=aliases,
            compiler_params=pltpu.CompilerParams(vmem_limit_bytes=vmem * MIB),
            cost_estimate=pl.CostEstimate(flops=0, bytes_accessed=0, transcendentals=0),
        )(*args, *chained)
        return results


def bf16_like(*shape):
    return jax.ShapeDtypeStruct(shape, bf16)


def f32_like(*shape):
    return jax.ShapeDtypeStruct(shape, f32)


def as_column(row):
    size = row.shape[1]
    diagonal = lax.broadcasted_iota(jnp.int32, (size, size), 0) == lax.broadcasted_iota(
        jnp.int32, (size, size), 1
    )
    return jnp.sum(jnp.where(diagonal, row, 0.0), axis=1, keepdims=True)


def as_row(column):
    size = column.shape[0]
    diagonal = lax.broadcasted_iota(jnp.int32, (size, size), 0) == lax.broadcasted_iota(
        jnp.int32, (size, size), 1
    )
    return jnp.sum(jnp.where(diagonal, column, 0.0), axis=0, keepdims=True)


def slot_rows(routing, experts, capacity):
    picks, tokens = routing.shape
    line = lax.broadcasted_iota(jnp.int32, (experts, tokens), 0)
    onehots = [(routing[k : k + 1] == line).astype(f32) for k in range(picks)]
    counted = functools.reduce(jnp.add, onehots)
    earlier = lax.broadcasted_iota(jnp.int32, (tokens, tokens), 0) < lax.broadcasted_iota(
        jnp.int32, (tokens, tokens), 1
    )
    before = jnp.dot(counted.astype(bf16), earlier.astype(bf16), preferred_element_type=f32)
    return [
        routing[k : k + 1].astype(f32) * capacity + jnp.sum(before * onehots[k], axis=0, keepdims=True)
        for k in range(picks)
    ]


def rows_for(first, count, slots, gates, dout):
    tokens = dout.shape[0]
    here = lax.broadcasted_iota(jnp.int32, (count, tokens), 0).astype(f32) + first
    hits = [here == row for row in slots]
    chosen = functools.reduce(jnp.logical_or, hits).astype(bf16)
    gate = functools.reduce(
        jnp.add, [jnp.sum(jnp.where(h, g, 0.0), axis=1, keepdims=True) for h, g in zip(hits, gates)]
    )
    return (jnp.dot(chosen, dout, preferred_element_type=f32) * gate).astype(bf16)


def pick_rows(first, slots_column, rows):
    lane = lax.broadcasted_iota(jnp.int32, (slots_column.shape[0], rows.shape[0]), 1).astype(f32)
    return jnp.dot((lane == slots_column - first).astype(bf16), rows, preferred_element_type=f32)


def message_body(capacity, routing_at, gates_at, dout_at, *refs):
    message_ref, *slot_refs = refs[:5]
    routing_ref, gates_ref, dout_ref, sems = refs[5:]
    moves = [
        pltpu.make_async_copy(a, b, sems.at[i])
        for i, (a, b) in enumerate(
            (
                (routing_at, routing_ref),
                (gates_at, gates_ref),
                (dout_at, dout_ref),
            )
        )
    ]
    for move in moves:
        move.start()
    for move in moves:
        move.wait()
    me = lax.axis_index("expert")
    picks, tokens = routing_ref.shape
    routing = routing_ref[...]
    slots = slot_rows(routing, LINE, capacity)
    gates = [gates_ref[k : k + 1] for k in range(picks)]
    dout = dout_ref[...]
    for m, ref in enumerate(slot_refs):
        first = ((me ^ m) * capacity).astype(f32)
        ref[...] = rows_for(first, capacity, slots, gates, dout)
    lines = []
    for k in range(picks):
        expert = routing[k : k + 1].astype(f32)
        lines += [expert, slots[k] - expert * capacity]
        left = gates[k]
        for _ in range(PIECES):
            piece = left.astype(bf16).astype(f32)
            lines.append(piece)
            left = left - piece
    lines.append(jnp.zeros((LANES - len(lines), tokens), f32))
    width = dout.shape[1]
    message_ref[:, :width] = dout
    message_ref[:, width:] = jnp.concatenate(lines, axis=0).T.astype(bf16)


def read_message(message_ref, picks, capacity):
    width = message_ref.shape[1] - LANES
    lines = message_ref[:, width:].astype(f32).T
    slots, gates = [], []
    for k in range(picks):
        at = k * (2 + PIECES)
        slots.append(lines[at : at + 1] * capacity + lines[at + 1 : at + 2])
        gates.append(jnp.sum(lines[at + 2 : at + 2 + PIECES], axis=0, keepdims=True))
    return slots, gates, message_ref[:, :width]


def rows_body(capacity, hidden_ref, weight_ref, *out_refs):
    me = lax.axis_index("expert")
    rows = jnp.concatenate([hidden_ref[me ^ m] for m in range(LINE)], axis=0)
    out = jnp.dot(rows, weight_ref[...], preferred_element_type=f32).astype(bf16)
    at = 0
    for ref in out_refs:
        ref[...] = out[at : at + ref.shape[0]]
        at += ref.shape[0]


def swap_body(*refs):
    own_ref, *arrived_refs, out_ref = refs
    count = own_ref.shape[0]
    out_ref[:count] = own_ref[...]
    for at, ref in enumerate(arrived_refs, 1):
        out_ref[at * count : (at + 1) * count] = ref[count:]


def relay_body(capacity, picks, message_ref, *out_refs):
    me = lax.axis_index("expert")
    slots, gates, dout = read_message(message_ref, picks, capacity)
    m = 0
    for ref in out_refs:
        for at in range(0, ref.shape[0], capacity):
            first = ((me ^ m) * capacity).astype(f32)
            ref[at : at + capacity] = rows_for(first, capacity, slots, gates, dout)
            m += 1


def rows_to_hidden(rows, weight_ref, grad_part):
    grad = lax.dot_general(
        rows, weight_ref[...], (((1,), (1,)), ((), ())), preferred_element_type=f32
    ).astype(bf16)
    capacity = grad_part[0][0].shape[1]
    for at, (ref, block) in enumerate(grad_part):
        ref[block] = grad[at * capacity : (at + 1) * capacity]


def cut_slices(rows, slice_refs):
    group = lax.axis_index("dp")
    width = slice_refs[0].shape[1]
    for d, part in enumerate(slice_refs):
        part[...] = rows[:, pl.ds(pl.multiple_of((group ^ d) * width, width), width)]


def near_body(capacity, weight_ref, *refs):
    block_refs, grad_ref, slice_refs, rows = refs[:-6], refs[-6], refs[-5:-1], refs[-1]
    gather_blocks(capacity, block_refs, rows)
    rows_to_hidden(rows[...], weight_ref, [(grad_ref, m) for m in range(4)])
    cut_slices(rows, slice_refs)


def gather_blocks(capacity, refs, rows):
    if len(refs) == 4:
        parts = [(ref, 0) for ref in refs]
    else:
        own, hop, pair = refs
        parts = [(own, 0), (pair, 0), (hop, 0), (pair, capacity)]
    for at, (ref, start) in enumerate(parts):
        rows[at * capacity : (at + 1) * capacity] = ref[start : start + capacity]


def far_body(capacity, weight_ref, near_grad_ref, *refs):
    block_refs, grad_ref, slice_refs, rows = refs[:-6], refs[-6], refs[-5:-1], refs[-1]
    me = lax.axis_index("expert")
    gather_blocks(capacity, block_refs, rows)
    for m in range(4):
        grad_ref[me ^ m] = near_grad_ref[m]
    rows_to_hidden(rows[...], weight_ref, [(grad_ref, me ^ m) for m in range(4, LINE)])
    cut_slices(rows, slice_refs)


def pack_body(*refs):
    hidden_refs, (near_ref, far_ref) = refs[:SQUARE], refs[-2:]
    me = lax.axis_index("expert")
    for ref, first in ((near_ref, 0), (far_ref, 4)):
        rows = jnp.concatenate([h[me ^ (first + m)] for h in hidden_refs for m in range(4)], axis=0)
        ref[...] = rows.T


def weight_body(columns_ref, *refs):
    slice_refs, others, out_ref = refs[:SQUARE], refs[SQUARE : SQUARE + 1], refs[-1]
    rows = jnp.concatenate([s[...] for s in slice_refs], axis=0)
    total = jnp.dot(columns_ref[...], rows, preferred_element_type=f32)
    for other in others if len(refs) > SQUARE + 1 else ():
        total = total + other[...]
    out_ref[...] = total


def combine_body(capacity, routing_ref, gates_ref, dout_ref, *refs):
    *block_refs, combined_ref, grad_gates_ref, rows = refs
    me = lax.axis_index("expert")
    picks = gates_ref.shape[0]
    c = capacity
    slots = slot_rows(routing_ref[...] ^ me, LINE, c)
    if len(block_refs) == LINE:
        parts = [(ref, 0) for ref in block_refs]
    else:
        own, *hops, pair = block_refs
        parts = [(own, 0), (pair, 0)]
        for at, ref in enumerate(hops, 1):
            parts += [(ref, 0), (pair, at * c)]
    for at, (ref, start) in enumerate(parts):
        rows[at * c : (at + 1) * c] = ref[start : start + c]
    dout = dout_ref[...].astype(f32)
    total = 0.0
    for k in range(picks):
        picked = pick_rows(0.0, as_column(slots[k]), rows[...])
        total += as_column(gates_ref[k : k + 1]) * picked
        grad_gates_ref[k : k + 1] = as_row(jnp.sum(picked * dout, axis=1, keepdims=True))
    combined_ref[...] = total.astype(bf16)


class Plan:
    def __init__(self, **values):
        self.values = values
        self.moves = {}
        self.run = Steps()

    def move(self, name, source, axis, m):
        self.moves[name] = (source, axis, m)

    def value(self, name):
        if name not in self.values:
            source, axis, m = self.moves[name]
            size = lax.axis_size(axis)
            self.values[name] = lax.ppermute(
                self.value(source), axis, [(i, i ^ m) for i in range(size)]
            )
        return self.values[name]

    def step(self, body, outs, ins, waits=(), held=(), **options):
        n, w, h, o = len(ins), len(waits), len(held), len(outs)
        args = [self.value(name) for name in (*ins, *waits, *held)]

        def whole(*refs):
            rest = refs[n + w + h :]
            body(*refs[:n], *rest[:o], *rest[o + h :])

        results = self.run(
            whole,
            [*outs.values(), *(jax.ShapeDtypeStruct(a.shape, a.dtype) for a in args[n + w :])],
            args,
            anywhere=tuple(range(n, n + w)),
            aliases={n + w + k: o + k for k in range(h)},
            **options,
        )
        self.values.update(zip((*outs, *held), results))


def on_device(routing, gates, hidden, w_down, dout):
    capacity, units = hidden.shape[3:]
    width = w_down.shape[2]
    tokens, picks = routing.shape
    part = width // SQUARE
    plan = Plan(
        routing=routing.T, gates=gates.T, hidden=hidden[0, 0], weight=w_down[0], dout=dout
    )
    step, move = plan.step, plan.move

    def block(count):
        return bf16_like(count * capacity, width)

    slices = bf16_like(4 * capacity, part)
    rows_scratch = [pltpu.VMEM((4 * capacity, width), bf16)]

    move("peer1", "hidden", "dp", 1)
    move("peer2", "hidden", "dp", 2)
    move("peer3", "peer1", "dp", 2)
    move("from_afar", "message", "expert", 4)
    for m in (1, 2, 3):
        move(f"near{m}", f"slots{m}", "expert", m)
        move(f"far{m}", f"relay{m}", "expert", m)
        move(f"near_slice{m}", f"near_cut{m}", "dp", m)
        move(f"far_slice{m}", f"far_cut{m}", "dp", m)
    for m in (2, 4, 6):
        move(f"got{m}", f"rows{m}", "expert", m)
    move("last", "last_swap", "expert", 1)

    step(
        functools.partial(message_body, capacity),
        dict(message=bf16_like(tokens, width + LANES), **{f"slots{m}": block(1) for m in range(4)}),
        ["routing", "gates", "dout"],
        scratch=[
            pltpu.VMEM((picks, tokens), jnp.int32),
            pltpu.VMEM((picks, tokens), f32),
            pltpu.VMEM((tokens, width), bf16),
            pltpu.SemaphoreType.DMA((3,)),
        ],
        pinned=(0, 1, 2),
        vmem=VMEM_ALL,
    )

    def rows(**o):
        step(
            functools.partial(rows_body, capacity),
            dict(rows0=block(1), rows1=block(1), rows2=block(2), rows4=block(2), rows6=block(2)),
            ["hidden", "weight"],
            **o,
        )

    def near(**o):
        step(
            functools.partial(near_body, capacity),
            dict(near_grad=bf16_like(4, capacity, units), **{f"near_cut{d}": slices for d in range(SQUARE)}),
            ["weight", "slots0", "near1", "near2", "near3"],
            scratch=rows_scratch,
            **o,
        )

    def relay(**o):
        step(
            functools.partial(relay_body, capacity, picks),
            {f"relay{m}": block(1) for m in range(4)},
            ["from_afar"],
            **o,
        )

    def pack(**o):
        step(
            pack_body,
            dict(near_columns=bf16_like(units, SQUARE * 4 * capacity), far_columns=bf16_like(units, SQUARE * 4 * capacity)),
            ["hidden", "peer1", "peer2", "peer3"],
            **o,
        )

    def near_weight(**o):
        step(
            weight_body,
            dict(near_weight=f32_like(units, part)),
            ["near_columns", "near_cut0", "near_slice1", "near_slice2", "near_slice3"],
            **o,
        )

    def far(**o):
        step(
            functools.partial(far_body, capacity),
            dict(grad_hidden=bf16_like(LINE, capacity, units), **{f"far_cut{d}": slices for d in range(SQUARE)}),
            ["weight", "near_grad", "relay0", "far1", "far2", "far3"],
            scratch=rows_scratch,
            **o,
        )

    def far_weight(**o):
        step(
            weight_body,
            dict(grad_down=f32_like(units, part)),
            ["far_columns", "far_cut0", "far_slice1", "far_slice2", "far_slice3", "near_weight"],
            **o,
        )

    def last_swap(**o):
        step(swap_body, dict(last_swap=block(4)), ["rows1", "got2", "got4", "got6"], **o)

    def combine(**o):
        step(
            functools.partial(combine_body, capacity),
            dict(combined=bf16_like(tokens, width), grad_gates=f32_like(picks, tokens)),
            ["routing", "gates", "dout", "rows0", "got2", "got4", "got6", "last"],
            scratch=[pltpu.VMEM((LINE * capacity, width), bf16)],
            **o,
        )

    rows()
    near()
    relay(waits=["near_slice1", "near_slice2"], held=["rows4", "rows6"])
    far(waits=["got6", "got2"])
    pack()
    near_weight()
    far_weight(waits=["got4"])
    last_swap()
    combine()
    v = plan.values
    return (v["combined"], v["grad_gates"].T, v["grad_hidden"][None, None], v["grad_down"][None])


def slot_index(routing, experts, capacity):
    flattened = routing.reshape(-1)
    onehot = (flattened[:, None] == jnp.arange(experts, dtype=jnp.int32)[None, :]).astype(jnp.int32)
    before = jnp.cumsum(onehot, axis=0) - onehot
    ranking = jnp.sum(before * onehot, axis=1)
    return flattened * capacity + ranking


def on_device_any(routing, gates, hidden, w_down, dout):
    experts = lax.axis_size("expert")
    capacity = hidden.shape[3]
    hidden_units = w_down.shape[1]
    model_width = w_down.shape[2]
    tok_rows = routing.shape[0]
    picks_per = routing.shape[1]
    weight = w_down[0]
    input_rows = hidden[0, 0].reshape(-1, hidden_units)
    outputs = jnp.dot(input_rows, weight, preferred_element_type=jnp.float32).astype(jnp.bfloat16)
    outputs = outputs.reshape(experts, capacity, model_width)
    returned = lax.all_to_all(outputs, "expert", split_axis=0, concat_axis=0, tiled=True)
    location = slot_index(routing, experts, capacity)
    picked = jnp.take(returned.reshape(experts * capacity, model_width), location, axis=0)
    picked = picked.reshape(tok_rows, picks_per, model_width).astype(jnp.float32)
    combined = jnp.sum(gates[..., None] * picked, axis=1).astype(jnp.bfloat16)
    grad_float = dout.astype(jnp.float32)
    grad_gates = jnp.sum(picked * grad_float[:, None, :], axis=2)
    scaled = (
        (gates[..., None] * grad_float[:, None, :]).astype(jnp.bfloat16).reshape(-1, model_width)
    )
    slot_grads = jnp.zeros((experts * capacity, model_width), jnp.bfloat16).at[location].set(scaled)
    slot_grads = slot_grads.reshape(experts, capacity, model_width)
    received = lax.all_to_all(slot_grads, "expert", split_axis=0, concat_axis=0, tiled=True)
    count_items = received.shape[1]
    flattened = received.reshape(-1, model_width)
    grad_rows = lax.dot_general(
        flattened, weight, (((1,), (1,)), ((), ())), preferred_element_type=jnp.float32
    )
    grad_hidden = grad_rows.astype(jnp.bfloat16).reshape(experts, count_items, hidden_units)
    arrived_rows = received.reshape(-1, model_width)
    partial_grad = lax.dot_general(
        input_rows, arrived_rows, (((0,), (0,)), ((), ())), preferred_element_type=jnp.float32
    )
    grad_down = lax.psum_scatter(
        partial_grad.astype(jnp.bfloat16), "dp", scatter_dimension=1, tiled=True
    ).astype(jnp.float32)
    return (combined, grad_gates, grad_hidden[None, None], grad_down[None])


def solution(mesh):
    placed = (
        P(("dp", "expert"), None),
        P(("dp", "expert"), None),
        P("dp", "expert", None, None, None),
        P("expert", None, None),
        P(("dp", "expert"), None),
    )
    planned = mesh.shape["expert"] == LINE and mesh.shape["dp"] == SQUARE
    return jax.shard_map(
        on_device if planned else on_device_any,
        mesh=mesh,
        in_specs=placed,
        out_specs=(
            P(("dp", "expert"), None),
            P(("dp", "expert"), None),
            P("dp", "expert", None, None, None),
            P("expert", None, "dp"),
        ),
        check_vma=False,
    )
```

```python
import functools

import jax
import jax.numpy as jnp
from jax import lax
from jax.experimental import pallas as pl
from jax.experimental.pallas import tpu as pltpu
from jax.sharding import PartitionSpec as P

LINE = 8
SQUARE = 4
LANES = 128
PIECES = 3
MIB = 1 << 20
VMEM_ALL = 60
f32, bf16 = jnp.float32, jnp.bfloat16


class Steps:
    def __init__(self):
        self.token = None

    def __call__(self, body, outs, args, scratch=(), vmem=40, aliases=None, anywhere=(), anywhere_out=(), pinned=()):
        aliases = aliases or {}
        whole = pl.BlockSpec(memory_space=pltpu.VMEM)
        free = pl.BlockSpec(memory_space=pl.ANY)
        fixed = pl.BlockSpec(memory_space=pltpu.HBM)
        in_specs = [
            fixed if i in pinned else free if i in aliases or i in anywhere else whole
            for i in range(len(args))
        ]
        out_specs = [free if o in aliases.values() or o in anywhere_out else whole for o in range(len(outs))]
        n_args, n_outs = len(args), len(outs)
        chained = () if self.token is None else (self.token,)

        def kernel(*refs):
            rest = refs[n_args + len(chained) :]
            body(*refs[:n_args], *rest[:n_outs], *rest[n_outs + 1 :])

        *results, self.token = pl.pallas_call(
            kernel,
            out_shape=[*outs, jax.ShapeDtypeStruct((8, LANES), f32)],
            in_specs=in_specs + [free] * len(chained),
            out_specs=out_specs + [free],
            scratch_shapes=scratch,
            input_output_aliases=aliases,
            compiler_params=pltpu.CompilerParams(vmem_limit_bytes=vmem * MIB),
            cost_estimate=pl.CostEstimate(flops=0, bytes_accessed=0, transcendentals=0),
        )(*args, *chained)
        return results


def bf16_like(*shape):
    return jax.ShapeDtypeStruct(shape, bf16)


def f32_like(*shape):
    return jax.ShapeDtypeStruct(shape, f32)


def as_column(row):
    size = row.shape[1]
    diagonal = lax.broadcasted_iota(jnp.int32, (size, size), 0) == lax.broadcasted_iota(
        jnp.int32, (size, size), 1
    )
    return jnp.sum(jnp.where(diagonal, row, 0.0), axis=1, keepdims=True)


def as_row(column):
    size = column.shape[0]
    diagonal = lax.broadcasted_iota(jnp.int32, (size, size), 0) == lax.broadcasted_iota(
        jnp.int32, (size, size), 1
    )
    return jnp.sum(jnp.where(diagonal, column, 0.0), axis=0, keepdims=True)


def slot_rows(routing, experts, capacity):
    picks, tokens = routing.shape
    line = lax.broadcasted_iota(jnp.int32, (experts, tokens), 0)
    onehots = [(routing[k : k + 1] == line).astype(f32) for k in range(picks)]
    counted = functools.reduce(jnp.add, onehots)
    earlier = lax.broadcasted_iota(jnp.int32, (tokens, tokens), 0) < lax.broadcasted_iota(
        jnp.int32, (tokens, tokens), 1
    )
    before = jnp.dot(counted.astype(bf16), earlier.astype(bf16), preferred_element_type=f32)
    return [
        routing[k : k + 1].astype(f32) * capacity + jnp.sum(before * onehots[k], axis=0, keepdims=True)
        for k in range(picks)
    ]


def rows_for(first, count, slots, gates, dout):
    tokens = dout.shape[0]
    here = lax.broadcasted_iota(jnp.int32, (count, tokens), 0).astype(f32) + first
    hits = [here == row for row in slots]
    chosen = functools.reduce(jnp.logical_or, hits).astype(bf16)
    gate = functools.reduce(
        jnp.add, [jnp.sum(jnp.where(h, g, 0.0), axis=1, keepdims=True) for h, g in zip(hits, gates)]
    )
    return (jnp.dot(chosen, dout, preferred_element_type=f32) * gate).astype(bf16)


def pick_rows(first, slots_column, rows):
    lane = lax.broadcasted_iota(jnp.int32, (slots_column.shape[0], rows.shape[0]), 1).astype(f32)
    return jnp.dot((lane == slots_column - first).astype(bf16), rows, preferred_element_type=f32)


def start_body(capacity, routing_at, gates_at, dout_at, hidden_at, weight_at, *refs):
    message_ref, give_refs, (near_own, near_pair, near_two, hidden_copy) = refs[0], refs[1:5], refs[5:9]
    routing_ref, gates_ref, dout_ref, hidden_ref, weight_ref, sems = refs[9:]
    moves = [
        pltpu.make_async_copy(a, b, sems.at[i])
        for i, (a, b) in enumerate(
            (
                (routing_at, routing_ref),
                (gates_at, gates_ref),
                (dout_at, dout_ref),
                (hidden_at, hidden_ref),
                (weight_at, weight_ref),
            )
        )
    ]
    for move in moves:
        move.start()
    me = lax.axis_index("expert")
    c = capacity
    picks, tokens = routing_ref.shape
    for move in moves[:3]:
        move.wait()
    routing = routing_ref[...]
    slots = slot_rows(routing, LINE, c)
    gates = [gates_ref[k : k + 1] for k in range(picks)]
    dout = dout_ref[...]
    lines = []
    for k in range(picks):
        expert = routing[k : k + 1].astype(f32)
        lines += [expert, slots[k] - expert * c]
        left = gates[k]
        for _ in range(PIECES):
            piece = left.astype(bf16).astype(f32)
            lines.append(piece)
            left = left - piece
    lines.append(jnp.zeros((LANES - len(lines), tokens), f32))
    width = dout.shape[1]
    message_ref[:, :width] = dout
    message_ref[:, width:] = jnp.concatenate(lines, axis=0).T.astype(bf16)
    for m, ref in enumerate(give_refs):
        first = ((me ^ m) * c).astype(f32)
        ref[:c] = rows_for(first, c, slots, gates, dout)
    moves[3].wait()
    hidden_copy[...] = hidden_ref[...]
    rows = jnp.concatenate([hidden_ref[me ^ m] for m in (4, 5, 6, 7, 0, 1, 3, 2)], axis=0)
    moves[4].wait()
    out = jnp.dot(rows, weight_ref[...], preferred_element_type=f32).astype(bf16)
    for m, ref in enumerate(give_refs):
        ref[c:] = out[m * c : (m + 1) * c]
    near_own[...] = out[4 * c : 5 * c]
    near_pair[...] = out[5 * c : 7 * c]
    near_two[...] = out[7 * c :]


def message_lines(message_ref, picks):
    width = message_ref.shape[1] - LANES
    lines = message_ref[:, width:].astype(f32).T
    experts, ranks, gates = [], [], []
    for k in range(picks):
        at = k * (2 + PIECES)
        experts.append(lines[at : at + 1])
        ranks.append(lines[at + 1 : at + 2])
        gates.append(jnp.sum(lines[at + 2 : at + 2 + PIECES], axis=0, keepdims=True))
    return experts, ranks, gates, message_ref[:, :width]


def read_message(message_ref, picks, capacity):
    experts, ranks, gates, dout = message_lines(message_ref, picks)
    return [e * capacity + r for e, r in zip(experts, ranks)], gates, dout


def relay_body(capacity, picks, message_ref, *out_refs):
    me = lax.axis_index("expert")
    slots, gates, dout = read_message(message_ref, picks, capacity)
    m = 0
    for ref in out_refs:
        for at in range(0, ref.shape[0], capacity):
            first = ((me ^ m) * capacity).astype(f32)
            ref[at : at + capacity] = rows_for(first, capacity, slots, gates, dout)
            m += 1


def rows_to_hidden(rows, weight_ref, grad_part):
    grad = lax.dot_general(
        rows, weight_ref[...], (((1,), (1,)), ((), ())), preferred_element_type=f32
    ).astype(bf16)
    capacity = grad_part[0][0].shape[1]
    for at, (ref, block) in enumerate(grad_part):
        ref[block] = grad[at * capacity : (at + 1) * capacity]


def cut_slices(rows, slice_refs):
    group = lax.axis_index("dp")
    width = slice_refs[0].shape[1]
    for d, part in enumerate(slice_refs):
        part[...] = rows[:, pl.ds(pl.multiple_of((group ^ d) * width, width), width)]


def near_body(capacity, weight_ref, *refs):
    block_refs, grad_ref, slice_refs, rows = refs[:-6], refs[-6], refs[-5:-1], refs[-1]
    gather_blocks(capacity, block_refs, rows)
    rows_to_hidden(rows[...], weight_ref, [(grad_ref, m) for m in range(4)])
    cut_slices(rows, slice_refs)


def gather_blocks(capacity, refs, rows, start=0):
    for at, ref in enumerate(refs):
        rows[at * capacity : (at + 1) * capacity] = ref[start : start + capacity]


def far_body(capacity, weight_ref, near_grad_ref, *refs):
    block_refs, grad_ref, slice_refs, rows = refs[:-6], refs[-6], refs[-5:-1], refs[-1]
    me = lax.axis_index("expert")
    gather_blocks(capacity, block_refs, rows)
    for m in range(4):
        grad_ref[me ^ m] = near_grad_ref[m]
    rows_to_hidden(rows[...], weight_ref, [(grad_ref, me ^ m) for m in range(4, LINE)])
    cut_slices(rows, slice_refs)


def pack_body(*refs):
    hidden_refs, (near_ref, far_ref) = refs[:SQUARE], refs[-2:]
    me = lax.axis_index("expert")
    for ref, first in ((near_ref, 0), (far_ref, 4)):
        rows = jnp.concatenate([h[me ^ (first + m)] for h in hidden_refs for m in range(4)], axis=0)
        ref[...] = rows.T


def weight_body(columns_ref, *refs):
    slice_refs, others, out_ref = refs[:SQUARE], refs[SQUARE : SQUARE + 1], refs[-1]
    rows = jnp.concatenate([s[...] for s in slice_refs], axis=0)
    total = jnp.dot(columns_ref[...], rows, preferred_element_type=f32)
    for other in others if len(refs) > SQUARE + 1 else ():
        total = total + other[...]
    out_ref[...] = total


def share_body(capacity, own_ref, pair_ref, out_ref):
    out_ref[:capacity] = own_ref[...]
    out_ref[capacity:] = pair_ref[capacity:]


def blend(capacity, experts, ranks, gates, dout, rows):
    me = lax.axis_index("expert")
    dout = dout.astype(f32)
    total, products = 0.0, []
    for expert, rank, gate in zip(experts, ranks, gates):
        block = (expert.astype(jnp.int32) ^ me).astype(f32)
        picked = pick_rows(0.0, as_column(block * capacity + rank), rows)
        total += as_column(gate) * picked
        products.append(jnp.sum(picked * dout, axis=1, keepdims=True))
    return total, products


def blend_body(capacity, picks, message_ref, *refs):
    *block_refs, out_ref, rows = refs
    gather_blocks(capacity, block_refs, rows, capacity)
    experts, ranks, gates, dout = message_lines(message_ref, picks)
    total, products = blend(capacity, experts, ranks, gates, dout, rows[...])
    width = dout.shape[1]
    out_ref[:, :width] = total.astype(bf16)
    lane = lax.broadcasted_iota(jnp.int32, (total.shape[0], LANES), 1)
    beside = jnp.zeros(lane.shape, f32)
    at = 0
    for left in products:
        for _ in range(PIECES):
            piece = left.astype(bf16).astype(f32)
            beside = jnp.where(lane == at, piece, beside)
            left = left - piece
            at += 1
    out_ref[:, width:] = beside.astype(bf16)


def combine_body(capacity, message_ref, own_ref, pair_ref, hop_ref, far_ref, *refs):
    combined_ref, grad_gates_ref, rows = refs
    c = capacity
    picks = grad_gates_ref.shape[0]
    rows[:c] = own_ref[...]
    rows[c : 2 * c] = pair_ref[:c]
    rows[2 * c :] = hop_ref[...]
    experts, ranks, gates, dout = message_lines(message_ref, picks)
    total, products = blend(c, experts, ranks, gates, dout, rows[...])
    width = dout.shape[1]
    combined_ref[...] = (total + far_ref[:, :width].astype(f32)).astype(bf16)
    beside = far_ref[:, width:].astype(f32)
    for k, near in enumerate(products):
        far = jnp.sum(beside[:, k * PIECES : (k + 1) * PIECES], axis=1, keepdims=True)
        grad_gates_ref[k : k + 1] = as_row(near + far)


class Plan:
    def __init__(self, **values):
        self.values = values
        self.moves = {}
        self.run = Steps()

    def move(self, name, source, axis, m):
        self.moves[name] = (source, axis, m)

    def value(self, name):
        if name not in self.values:
            source, axis, m = self.moves[name]
            size = lax.axis_size(axis)
            self.values[name] = lax.ppermute(
                self.value(source), axis, [(i, i ^ m) for i in range(size)]
            )
        return self.values[name]

    def step(self, body, outs, ins, waits=(), held=(), **options):
        n, w, h, o = len(ins), len(waits), len(held), len(outs)
        args = [self.value(name) for name in (*ins, *waits, *held)]

        def whole(*refs):
            rest = refs[n + w + h :]
            body(*refs[:n], *rest[:o], *rest[o + h :])

        results = self.run(
            whole,
            [*outs.values(), *(jax.ShapeDtypeStruct(a.shape, a.dtype) for a in args[n + w :])],
            args,
            anywhere=tuple(range(n, n + w)),
            aliases={n + w + k: o + k for k in range(h)},
            **options,
        )
        self.values.update(zip((*outs, *held), results))


def on_device(routing, gates, hidden, w_down, dout):
    capacity, units = hidden.shape[3:]
    width = w_down.shape[2]
    tokens, picks = routing.shape
    part = width // SQUARE
    plan = Plan(
        routing=routing.T, gates=gates.T, hidden=hidden[0, 0], weight=w_down[0], dout=dout
    )
    step, move = plan.step, plan.move

    def block(count):
        return bf16_like(count * capacity, width)

    slices = bf16_like(4 * capacity, part)
    rows_scratch = [pltpu.VMEM((4 * capacity, width), bf16)]

    move("peer1", "hidden_copy", "dp", 1)
    move("peer2", "hidden_copy", "dp", 2)
    move("peer3", "peer1", "dp", 2)
    move("from_afar", "message", "expert", 4)
    for m in (1, 2, 3):
        move(f"near{m}", f"give{m}", "expert", m)
        move(f"far{m}", f"relay{m}", "expert", m)
        move(f"near_slice{m}", f"near_cut{m}", "dp", m)
        move(f"far_slice{m}", f"far_cut{m}", "dp", m)
    move("pair_near", "rows_near", "expert", 1)
    move("hop_near", "share_near", "expert", 2)
    move("blended", "blend", "expert", 4)

    step(
        functools.partial(start_body, capacity),
        dict(
            message=bf16_like(tokens, width + LANES),
            **{f"give{m}": block(2) for m in range(4)},
            rows0=block(1),
            rows_near=block(2),
            rows2=block(1),
            hidden_copy=bf16_like(LINE, capacity, units),
        ),
        ["routing", "gates", "dout", "hidden", "weight"],
        scratch=[
            pltpu.VMEM((picks, tokens), jnp.int32),
            pltpu.VMEM((picks, tokens), f32),
            pltpu.VMEM((tokens, width), bf16),
            pltpu.VMEM((LINE, capacity, units), bf16),
            pltpu.VMEM((units, width), bf16),
            pltpu.SemaphoreType.DMA((5,)),
        ],
        pinned=(0, 1, 2, 3, 4),
        vmem=VMEM_ALL,
    )

    def near(**o):
        step(
            functools.partial(near_body, capacity),
            dict(near_grad=bf16_like(4, capacity, units), **{f"near_cut{d}": slices for d in range(SQUARE)}),
            ["weight", "give0", "near1", "near2", "near3"],
            scratch=rows_scratch,
            **o,
        )

    def relay(**o):
        step(
            functools.partial(relay_body, capacity, picks),
            {f"relay{m}": block(1) for m in range(4)},
            ["from_afar"],
            **o,
        )

    def pack(**o):
        step(
            pack_body,
            dict(near_columns=bf16_like(units, SQUARE * 4 * capacity), far_columns=bf16_like(units, SQUARE * 4 * capacity)),
            ["hidden", "peer1", "peer2", "peer3"],
            **o,
        )

    def near_weight(**o):
        step(
            weight_body,
            dict(near_weight=f32_like(units, part)),
            ["near_columns", "near_cut0", "near_slice1", "near_slice2", "near_slice3"],
            **o,
        )

    def far(**o):
        step(
            functools.partial(far_body, capacity),
            dict(grad_hidden=bf16_like(LINE, capacity, units), **{f"far_cut{d}": slices for d in range(SQUARE)}),
            ["weight", "near_grad", "relay0", "far1", "far2", "far3"],
            scratch=rows_scratch,
            **o,
        )

    def far_weight(**o):
        step(
            weight_body,
            dict(grad_down=f32_like(units, part)),
            ["far_columns", "far_cut0", "far_slice1", "far_slice2", "far_slice3", "near_weight"],
            **o,
        )

    def share(name, own, **o):
        step(
            functools.partial(share_body, capacity),
            {f"share_{name}": block(2)},
            [own, f"pair_{name}"],
            **o,
        )

    def gate(*waits, held=()):
        step(lambda *_: None, {}, [], waits=waits, held=held)

    def blend(**o):
        step(
            functools.partial(blend_body, capacity, picks),
            dict(blend=bf16_like(tokens, width + LANES)),
            ["from_afar", "give0", "near1", "near2", "near3"],
            scratch=rows_scratch,
            **o,
        )

    def combine(**o):
        step(
            functools.partial(combine_body, capacity),
            dict(combined=bf16_like(tokens, width), grad_gates=f32_like(picks, tokens)),
            ["message", "rows0", "pair_near", "hop_near", "blended"],
            scratch=rows_scratch,
            **o,
        )

    gate("near1")
    relay(waits=["peer1", "peer2"])
    near()
    blend()
    share("near", "rows2")
    far()
    pack()
    near_weight()
    far_weight()
    combine()
    v = plan.values
    return (v["combined"], v["grad_gates"].T, v["grad_hidden"][None, None], v["grad_down"][None])


def slot_index(routing, experts, capacity):
    flattened = routing.reshape(-1)
    onehot = (flattened[:, None] == jnp.arange(experts, dtype=jnp.int32)[None, :]).astype(jnp.int32)
    before = jnp.cumsum(onehot, axis=0) - onehot
    ranking = jnp.sum(before * onehot, axis=1)
    return flattened * capacity + ranking


def on_device_any(routing, gates, hidden, w_down, dout):
    experts = lax.axis_size("expert")
    capacity = hidden.shape[3]
    hidden_units = w_down.shape[1]
    model_width = w_down.shape[2]
    tok_rows = routing.shape[0]
    picks_per = routing.shape[1]
    weight = w_down[0]
    input_rows = hidden[0, 0].reshape(-1, hidden_units)
    outputs = jnp.dot(input_rows, weight, preferred_element_type=jnp.float32).astype(jnp.bfloat16)
    outputs = outputs.reshape(experts, capacity, model_width)
    returned = lax.all_to_all(outputs, "expert", split_axis=0, concat_axis=0, tiled=True)
    location = slot_index(routing, experts, capacity)
    picked = jnp.take(returned.reshape(experts * capacity, model_width), location, axis=0)
    picked = picked.reshape(tok_rows, picks_per, model_width).astype(jnp.float32)
    combined = jnp.sum(gates[..., None] * picked, axis=1).astype(jnp.bfloat16)
    grad_float = dout.astype(jnp.float32)
    grad_gates = jnp.sum(picked * grad_float[:, None, :], axis=2)
    scaled = (
        (gates[..., None] * grad_float[:, None, :]).astype(jnp.bfloat16).reshape(-1, model_width)
    )
    slot_grads = jnp.zeros((experts * capacity, model_width), jnp.bfloat16).at[location].set(scaled)
    slot_grads = slot_grads.reshape(experts, capacity, model_width)
    received = lax.all_to_all(slot_grads, "expert", split_axis=0, concat_axis=0, tiled=True)
    count_items = received.shape[1]
    flattened = received.reshape(-1, model_width)
    grad_rows = lax.dot_general(
        flattened, weight, (((1,), (1,)), ((), ())), preferred_element_type=jnp.float32
    )
    grad_hidden = grad_rows.astype(jnp.bfloat16).reshape(experts, count_items, hidden_units)
    arrived_rows = received.reshape(-1, model_width)
    partial_grad = lax.dot_general(
        input_rows, arrived_rows, (((0,), (0,)), ((), ())), preferred_element_type=jnp.float32
    )
    grad_down = lax.psum_scatter(
        partial_grad.astype(jnp.bfloat16), "dp", scatter_dimension=1, tiled=True
    ).astype(jnp.float32)
    return (combined, grad_gates, grad_hidden[None, None], grad_down[None])


def solution(mesh):
    placed = (
        P(("dp", "expert"), None),
        P(("dp", "expert"), None),
        P("dp", "expert", None, None, None),
        P("expert", None, None),
        P(("dp", "expert"), None),
    )
    planned = mesh.shape["expert"] == LINE and mesh.shape["dp"] == SQUARE
    return jax.shard_map(
        on_device if planned else on_device_any,
        mesh=mesh,
        in_specs=placed,
        out_specs=(
            P(("dp", "expert"), None),
            P(("dp", "expert"), None),
            P("dp", "expert", None, None, None),
            P("expert", None, "dp"),
        ),
        check_vma=False,
    )
```

```python
import functools

import jax
import jax.numpy as jnp
from jax import lax
from jax.experimental import pallas as pl
from jax.experimental.pallas import tpu as pltpu
from jax.sharding import PartitionSpec as P

LINE = 8
SQUARE = 4
LANES = 128
PIECES = 3
MIB = 1 << 20
VMEM_ALL = 60
f32, bf16 = jnp.float32, jnp.bfloat16


class Steps:
    def __init__(self):
        self.token = None

    def __call__(self, body, outs, args, scratch=(), vmem=40, aliases=None, anywhere=(), pinned=()):
        aliases = aliases or {}
        whole = pl.BlockSpec(memory_space=pltpu.VMEM)
        free = pl.BlockSpec(memory_space=pl.ANY)
        fixed = pl.BlockSpec(memory_space=pltpu.HBM)
        in_specs = [
            fixed if i in pinned else free if i in aliases or i in anywhere else whole
            for i in range(len(args))
        ]
        out_specs = [free if o in aliases.values() else whole for o in range(len(outs))]
        n_args, n_outs = len(args), len(outs)
        chained = () if self.token is None else (self.token,)

        def kernel(*refs):
            rest = refs[n_args + len(chained) :]
            body(*refs[:n_args], *rest[:n_outs], *rest[n_outs + 1 :])

        *results, self.token = pl.pallas_call(
            kernel,
            out_shape=[*outs, jax.ShapeDtypeStruct((8, LANES), f32)],
            in_specs=in_specs + [free] * len(chained),
            out_specs=out_specs + [free],
            scratch_shapes=scratch,
            input_output_aliases=aliases,
            compiler_params=pltpu.CompilerParams(vmem_limit_bytes=vmem * MIB),
            cost_estimate=pl.CostEstimate(flops=0, bytes_accessed=0, transcendentals=0),
        )(*args, *chained)
        return results


def bf16_like(*shape):
    return jax.ShapeDtypeStruct(shape, bf16)


def f32_like(*shape):
    return jax.ShapeDtypeStruct(shape, f32)


def as_column(row):
    size = row.shape[1]
    diagonal = lax.broadcasted_iota(jnp.int32, (size, size), 0) == lax.broadcasted_iota(
        jnp.int32, (size, size), 1
    )
    return jnp.sum(jnp.where(diagonal, row, 0.0), axis=1, keepdims=True)


def as_row(column):
    size = column.shape[0]
    diagonal = lax.broadcasted_iota(jnp.int32, (size, size), 0) == lax.broadcasted_iota(
        jnp.int32, (size, size), 1
    )
    return jnp.sum(jnp.where(diagonal, column, 0.0), axis=0, keepdims=True)


def slot_rows(routing, experts, capacity):
    picks, tokens = routing.shape
    line = lax.broadcasted_iota(jnp.int32, (experts, tokens), 0)
    onehots = [(routing[k : k + 1] == line).astype(f32) for k in range(picks)]
    counted = functools.reduce(jnp.add, onehots)
    earlier = lax.broadcasted_iota(jnp.int32, (tokens, tokens), 0) < lax.broadcasted_iota(
        jnp.int32, (tokens, tokens), 1
    )
    before = jnp.dot(counted.astype(bf16), earlier.astype(bf16), preferred_element_type=f32)
    return [
        routing[k : k + 1].astype(f32) * capacity + jnp.sum(before * onehots[k], axis=0, keepdims=True)
        for k in range(picks)
    ]


def rows_for(first, count, slots, gates, dout):
    tokens = dout.shape[0]
    here = lax.broadcasted_iota(jnp.int32, (count, tokens), 0).astype(f32) + first
    hits = [here == row for row in slots]
    chosen = functools.reduce(jnp.logical_or, hits).astype(bf16)
    gate = functools.reduce(
        jnp.add, [jnp.sum(jnp.where(h, g, 0.0), axis=1, keepdims=True) for h, g in zip(hits, gates)]
    )
    return (jnp.dot(chosen, dout, preferred_element_type=f32) * gate).astype(bf16)


def pick_rows(first, slots_column, rows):
    lane = lax.broadcasted_iota(jnp.int32, (slots_column.shape[0], rows.shape[0]), 1).astype(f32)
    return jnp.dot((lane == slots_column - first).astype(bf16), rows, preferred_element_type=f32)


def start_body(capacity, routing_at, gates_at, dout_at, hidden_at, weight_at, *refs):
    message_ref, give_refs = refs[0], refs[1:5]
    routing_ref, gates_ref, dout_ref, hidden_ref, weight_ref, sems = refs[5:]
    moves = [
        pltpu.make_async_copy(a, b, sems.at[i])
        for i, (a, b) in enumerate(
            (
                (routing_at, routing_ref),
                (gates_at, gates_ref),
                (dout_at, dout_ref),
                (hidden_at, hidden_ref),
                (weight_at, weight_ref),
            )
        )
    ]
    for move in moves:
        move.start()
    me = lax.axis_index("expert")
    c = capacity
    picks, tokens = routing_ref.shape
    for move in moves[:3]:
        move.wait()
    routing = routing_ref[...]
    slots = slot_rows(routing, LINE, c)
    gates = [gates_ref[k : k + 1] for k in range(picks)]
    dout = dout_ref[...]
    lines = []
    for k in range(picks):
        expert = routing[k : k + 1].astype(f32)
        lines += [expert, slots[k] - expert * c]
        left = gates[k]
        for _ in range(PIECES):
            piece = left.astype(bf16).astype(f32)
            lines.append(piece)
            left = left - piece
    lines.append(jnp.zeros((LANES - len(lines), tokens), f32))
    width = dout.shape[1]
    message_ref[:, :width] = dout
    message_ref[:, width:] = jnp.concatenate(lines, axis=0).T.astype(bf16)
    for m, ref in enumerate(give_refs):
        first = ((me ^ m) * c).astype(f32)
        ref[:c] = rows_for(first, c, slots, gates, dout)
    moves[3].wait()
    rows = jnp.concatenate([hidden_ref[me ^ m] for m in range(4, LINE)], axis=0)
    moves[4].wait()
    out = jnp.dot(rows, weight_ref[...], preferred_element_type=f32).astype(bf16)
    for m, ref in enumerate(give_refs):
        ref[c:] = out[m * c : (m + 1) * c]


def rest_body(hidden_ref, weight_ref, *refs):
    *out_refs, hidden_copy = refs
    me = lax.axis_index("expert")
    rows = jnp.concatenate([hidden_ref[me ^ m] for m in (0, 1, 3, 2)], axis=0)
    out = jnp.dot(rows, weight_ref[...], preferred_element_type=f32).astype(bf16)
    at = 0
    for ref in out_refs:
        ref[...] = out[at : at + ref.shape[0]]
        at += ref.shape[0]
    hidden_copy[...] = hidden_ref[...]


def message_lines(message_ref, picks):
    width = message_ref.shape[1] - LANES
    lines = message_ref[:, width:].astype(f32).T
    experts, ranks, gates = [], [], []
    for k in range(picks):
        at = k * (2 + PIECES)
        experts.append(lines[at : at + 1])
        ranks.append(lines[at + 1 : at + 2])
        gates.append(jnp.sum(lines[at + 2 : at + 2 + PIECES], axis=0, keepdims=True))
    return experts, ranks, gates, message_ref[:, :width]


def read_message(message_ref, picks, capacity):
    experts, ranks, gates, dout = message_lines(message_ref, picks)
    return [e * capacity + r for e, r in zip(experts, ranks)], gates, dout


def relay_body(capacity, picks, message_ref, *out_refs):
    me = lax.axis_index("expert")
    slots, gates, dout = read_message(message_ref, picks, capacity)
    m = 0
    for ref in out_refs:
        for at in range(0, ref.shape[0], capacity):
            first = ((me ^ m) * capacity).astype(f32)
            ref[at : at + capacity] = rows_for(first, capacity, slots, gates, dout)
            m += 1


def rows_to_hidden(rows, weight_ref, grad_part):
    grad = lax.dot_general(
        rows, weight_ref[...], (((1,), (1,)), ((), ())), preferred_element_type=f32
    ).astype(bf16)
    capacity = grad_part[0][0].shape[1]
    for at, (ref, block) in enumerate(grad_part):
        ref[block] = grad[at * capacity : (at + 1) * capacity]


def cut_slices(rows, slice_refs):
    group = lax.axis_index("dp")
    width = slice_refs[0].shape[1]
    for d, part in enumerate(slice_refs):
        part[...] = rows[:, pl.ds(pl.multiple_of((group ^ d) * width, width), width)]


def near_body(capacity, weight_ref, *refs):
    block_refs, grad_ref, slice_refs, rows = refs[:-6], refs[-6], refs[-5:-1], refs[-1]
    gather_blocks(capacity, block_refs, rows)
    rows_to_hidden(rows[...], weight_ref, [(grad_ref, m) for m in range(4)])
    cut_slices(rows, slice_refs)


def gather_blocks(capacity, refs, rows, start=0):
    for at, ref in enumerate(refs):
        rows[at * capacity : (at + 1) * capacity] = ref[start : start + capacity]


def far_body(capacity, weight_ref, near_grad_ref, *refs):
    block_refs, grad_ref, slice_refs, rows = refs[:-6], refs[-6], refs[-5:-1], refs[-1]
    me = lax.axis_index("expert")
    gather_blocks(capacity, block_refs, rows)
    for m in range(4):
        grad_ref[me ^ m] = near_grad_ref[m]
    rows_to_hidden(rows[...], weight_ref, [(grad_ref, me ^ m) for m in range(4, LINE)])
    cut_slices(rows, slice_refs)


def pack_body(*refs):
    hidden_refs, (near_ref, far_ref) = refs[:SQUARE], refs[-2:]
    me = lax.axis_index("expert")
    for ref, first in ((near_ref, 0), (far_ref, 4)):
        rows = jnp.concatenate([h[me ^ (first + m)] for h in hidden_refs for m in range(4)], axis=0)
        ref[...] = rows.T


def weight_body(columns_ref, *refs):
    slice_refs, others, out_ref = refs[:SQUARE], refs[SQUARE : SQUARE + 1], refs[-1]
    rows = jnp.concatenate([s[...] for s in slice_refs], axis=0)
    total = jnp.dot(columns_ref[...], rows, preferred_element_type=f32)
    for other in others if len(refs) > SQUARE + 1 else ():
        total = total + other[...]
    out_ref[...] = total


def share_body(capacity, own_ref, pair_ref, out_ref):
    out_ref[:capacity] = own_ref[...]
    out_ref[capacity:] = pair_ref[capacity:]


def blend(capacity, experts, ranks, gates, dout, rows):
    me = lax.axis_index("expert")
    dout = dout.astype(f32)
    total, products = 0.0, []
    for expert, rank, gate in zip(experts, ranks, gates):
        block = (expert.astype(jnp.int32) ^ me).astype(f32)
        picked = pick_rows(0.0, as_column(block * capacity + rank), rows)
        total += as_column(gate) * picked
        products.append(jnp.sum(picked * dout, axis=1, keepdims=True))
    return total, products


def blend_body(capacity, picks, message_ref, *refs):
    *block_refs, out_ref, rows = refs
    gather_blocks(capacity, block_refs, rows, capacity)
    experts, ranks, gates, dout = message_lines(message_ref, picks)
    total, products = blend(capacity, experts, ranks, gates, dout, rows[...])
    width = dout.shape[1]
    out_ref[:, :width] = total.astype(bf16)
    lane = lax.broadcasted_iota(jnp.int32, (total.shape[0], LANES), 1)
    beside = jnp.zeros(lane.shape, f32)
    at = 0
    for left in products:
        for _ in range(PIECES):
            piece = left.astype(bf16).astype(f32)
            beside = jnp.where(lane == at, piece, beside)
            left = left - piece
            at += 1
    out_ref[:, width:] = beside.astype(bf16)


def combine_body(capacity, message_ref, own_ref, pair_ref, hop_ref, far_ref, *refs):
    combined_ref, grad_gates_ref, rows = refs
    c = capacity
    picks = grad_gates_ref.shape[0]
    rows[:c] = own_ref[...]
    rows[c : 2 * c] = pair_ref[:c]
    rows[2 * c :] = hop_ref[...]
    experts, ranks, gates, dout = message_lines(message_ref, picks)
    total, products = blend(c, experts, ranks, gates, dout, rows[...])
    width = dout.shape[1]
    combined_ref[...] = (total + far_ref[:, :width].astype(f32)).astype(bf16)
    beside = far_ref[:, width:].astype(f32)
    for k, near in enumerate(products):
        far = jnp.sum(beside[:, k * PIECES : (k + 1) * PIECES], axis=1, keepdims=True)
        grad_gates_ref[k : k + 1] = as_row(near + far)


class Plan:
    def __init__(self, **values):
        self.values = values
        self.moves = {}
        self.run = Steps()

    def move(self, name, source, axis, m):
        self.moves[name] = (source, axis, m)

    def value(self, name):
        if name not in self.values:
            source, axis, m = self.moves[name]
            size = lax.axis_size(axis)
            self.values[name] = lax.ppermute(
                self.value(source), axis, [(i, i ^ m) for i in range(size)]
            )
        return self.values[name]

    def step(self, body, outs, ins, waits=(), held=(), **options):
        n, w, h, o = len(ins), len(waits), len(held), len(outs)
        args = [self.value(name) for name in (*ins, *waits, *held)]

        def whole(*refs):
            rest = refs[n + w + h :]
            body(*refs[:n], *rest[:o], *rest[o + h :])

        results = self.run(
            whole,
            [*outs.values(), *(jax.ShapeDtypeStruct(a.shape, a.dtype) for a in args[n + w :])],
            args,
            anywhere=tuple(range(n, n + w)),
            aliases={n + w + k: o + k for k in range(h)},
            **options,
        )
        self.values.update(zip((*outs, *held), results))


def on_device(routing, gates, hidden, w_down, dout):
    capacity, units = hidden.shape[3:]
    width = w_down.shape[2]
    tokens, picks = routing.shape
    part = width // SQUARE
    plan = Plan(
        routing=routing.T, gates=gates.T, hidden=hidden[0, 0], weight=w_down[0], dout=dout
    )
    step, move = plan.step, plan.move

    def block(count):
        return bf16_like(count * capacity, width)

    slices = bf16_like(4 * capacity, part)
    rows_scratch = [pltpu.VMEM((4 * capacity, width), bf16)]

    move("peer1", "hidden_copy", "dp", 1)
    move("peer2", "hidden_copy", "dp", 2)
    move("peer3", "peer1", "dp", 2)
    move("from_afar", "message", "expert", 4)
    for m in (1, 2, 3):
        move(f"near{m}", f"give{m}", "expert", m)
        move(f"far{m}", f"relay{m}", "expert", m)
        move(f"near_slice{m}", f"near_cut{m}", "dp", m)
        move(f"far_slice{m}", f"far_cut{m}", "dp", m)
    move("pair_near", "rows_near", "expert", 1)
    move("hop_near", "share_near", "expert", 2)
    move("blended", "blend", "expert", 4)

    step(
        functools.partial(start_body, capacity),
        dict(
            message=bf16_like(tokens, width + LANES),
            **{f"give{m}": block(2) for m in range(4)},
        ),
        ["routing", "gates", "dout", "hidden", "weight"],
        scratch=[
            pltpu.VMEM((picks, tokens), jnp.int32),
            pltpu.VMEM((picks, tokens), f32),
            pltpu.VMEM((tokens, width), bf16),
            pltpu.VMEM((LINE, capacity, units), bf16),
            pltpu.VMEM((units, width), bf16),
            pltpu.SemaphoreType.DMA((5,)),
        ],
        pinned=(0, 1, 2, 3, 4),
        vmem=VMEM_ALL,
    )

    def rest(**o):
        step(
            rest_body,
            dict(
                rows0=block(1),
                rows_near=block(2),
                rows2=block(1),
                hidden_copy=bf16_like(LINE, capacity, units),
            ),
            ["hidden", "weight"],
            **o,
        )

    def near(**o):
        step(
            functools.partial(near_body, capacity),
            dict(near_grad=bf16_like(4, capacity, units), **{f"near_cut{d}": slices for d in range(SQUARE)}),
            ["weight", "give0", "near1", "near2", "near3"],
            scratch=rows_scratch,
            **o,
        )

    def relay(**o):
        step(
            functools.partial(relay_body, capacity, picks),
            {f"relay{m}": block(1) for m in range(4)},
            ["from_afar"],
            **o,
        )

    def pack(**o):
        step(
            pack_body,
            dict(near_columns=bf16_like(units, SQUARE * 4 * capacity), far_columns=bf16_like(units, SQUARE * 4 * capacity)),
            ["hidden", "peer1", "peer2", "peer3"],
            **o,
        )

    def near_weight(**o):
        step(
            weight_body,
            dict(near_weight=f32_like(units, part)),
            ["near_columns", "near_cut0", "near_slice1", "near_slice2", "near_slice3"],
            **o,
        )

    def far(**o):
        step(
            functools.partial(far_body, capacity),
            dict(grad_hidden=bf16_like(LINE, capacity, units), **{f"far_cut{d}": slices for d in range(SQUARE)}),
            ["weight", "near_grad", "relay0", "far1", "far2", "far3"],
            scratch=rows_scratch,
            **o,
        )

    def far_weight(**o):
        step(
            weight_body,
            dict(grad_down=f32_like(units, part)),
            ["far_columns", "far_cut0", "far_slice1", "far_slice2", "far_slice3", "near_weight"],
            **o,
        )

    def share(name, own, **o):
        step(
            functools.partial(share_body, capacity),
            {f"share_{name}": block(2)},
            [own, f"pair_{name}"],
            **o,
        )

    def gate(*waits, held=()):
        step(lambda *_: None, {}, [], waits=waits, held=held)

    def blend(**o):
        step(
            functools.partial(blend_body, capacity, picks),
            dict(blend=bf16_like(tokens, width + LANES)),
            ["from_afar", "give0", "near1", "near2", "near3"],
            scratch=rows_scratch,
            **o,
        )

    def combine(**o):
        step(
            functools.partial(combine_body, capacity),
            dict(combined=bf16_like(tokens, width), grad_gates=f32_like(picks, tokens)),
            ["message", "rows0", "pair_near", "hop_near", "blended"],
            scratch=rows_scratch,
            **o,
        )

    rest(waits=["near1"])
    relay(waits=["peer1", "peer2"])
    near()
    blend()
    share("near", "rows2")
    far()
    pack()
    near_weight()
    far_weight()
    combine()
    v = plan.values
    return (v["combined"], v["grad_gates"].T, v["grad_hidden"][None, None], v["grad_down"][None])


def slot_index(routing, experts, capacity):
    flattened = routing.reshape(-1)
    onehot = (flattened[:, None] == jnp.arange(experts, dtype=jnp.int32)[None, :]).astype(jnp.int32)
    before = jnp.cumsum(onehot, axis=0) - onehot
    ranking = jnp.sum(before * onehot, axis=1)
    return flattened * capacity + ranking


def on_device_any(routing, gates, hidden, w_down, dout):
    experts = lax.axis_size("expert")
    capacity = hidden.shape[3]
    hidden_units = w_down.shape[1]
    model_width = w_down.shape[2]
    tok_rows = routing.shape[0]
    picks_per = routing.shape[1]
    weight = w_down[0]
    input_rows = hidden[0, 0].reshape(-1, hidden_units)
    outputs = jnp.dot(input_rows, weight, preferred_element_type=jnp.float32).astype(jnp.bfloat16)
    outputs = outputs.reshape(experts, capacity, model_width)
    returned = lax.all_to_all(outputs, "expert", split_axis=0, concat_axis=0, tiled=True)
    location = slot_index(routing, experts, capacity)
    picked = jnp.take(returned.reshape(experts * capacity, model_width), location, axis=0)
    picked = picked.reshape(tok_rows, picks_per, model_width).astype(jnp.float32)
    combined = jnp.sum(gates[..., None] * picked, axis=1).astype(jnp.bfloat16)
    grad_float = dout.astype(jnp.float32)
    grad_gates = jnp.sum(picked * grad_float[:, None, :], axis=2)
    scaled = (
        (gates[..., None] * grad_float[:, None, :]).astype(jnp.bfloat16).reshape(-1, model_width)
    )
    slot_grads = jnp.zeros((experts * capacity, model_width), jnp.bfloat16).at[location].set(scaled)
    slot_grads = slot_grads.reshape(experts, capacity, model_width)
    received = lax.all_to_all(slot_grads, "expert", split_axis=0, concat_axis=0, tiled=True)
    count_items = received.shape[1]
    flattened = received.reshape(-1, model_width)
    grad_rows = lax.dot_general(
        flattened, weight, (((1,), (1,)), ((), ())), preferred_element_type=jnp.float32
    )
    grad_hidden = grad_rows.astype(jnp.bfloat16).reshape(experts, count_items, hidden_units)
    arrived_rows = received.reshape(-1, model_width)
    partial_grad = lax.dot_general(
        input_rows, arrived_rows, (((0,), (0,)), ((), ())), preferred_element_type=jnp.float32
    )
    grad_down = lax.psum_scatter(
        partial_grad.astype(jnp.bfloat16), "dp", scatter_dimension=1, tiled=True
    ).astype(jnp.float32)
    return (combined, grad_gates, grad_hidden[None, None], grad_down[None])


def solution(mesh):
    placed = (
        P(("dp", "expert"), None),
        P(("dp", "expert"), None),
        P("dp", "expert", None, None, None),
        P("expert", None, None),
        P(("dp", "expert"), None),
    )
    planned = mesh.shape["expert"] == LINE and mesh.shape["dp"] == SQUARE
    return jax.shard_map(
        on_device if planned else on_device_any,
        mesh=mesh,
        in_specs=placed,
        out_specs=(
            P(("dp", "expert"), None),
            P(("dp", "expert"), None),
            P("dp", "expert", None, None, None),
            P("expert", None, "dp"),
        ),
        check_vma=False,
    )
```

```python
import functools

import jax
import jax.numpy as jnp
from jax import lax
from jax.experimental import pallas as pl
from jax.experimental.pallas import tpu as pltpu
from jax.sharding import PartitionSpec as P

LINE = 8
SQUARE = 4
LANES = 128
WEIGHT_PARTS = 3
PIECES = 3
MIB = 1 << 20
VMEM_ALL = 60
f32, bf16 = jnp.float32, jnp.bfloat16


class Steps:
    def __init__(self):
        self.token = None

    def __call__(self, body, outs, args, scratch=(), vmem=40, aliases=None, anywhere=(), pinned=()):
        aliases = aliases or {}
        whole = pl.BlockSpec(memory_space=pltpu.VMEM)
        free = pl.BlockSpec(memory_space=pl.ANY)
        fixed = pl.BlockSpec(memory_space=pltpu.HBM)
        in_specs = [
            fixed if i in pinned else free if i in aliases or i in anywhere else whole
            for i in range(len(args))
        ]
        out_specs = [free if o in aliases.values() else whole for o in range(len(outs))]
        n_args, n_outs = len(args), len(outs)
        chained = () if self.token is None else (self.token,)

        def kernel(*refs):
            rest = refs[n_args + len(chained) :]
            body(*refs[:n_args], *rest[:n_outs], *rest[n_outs + 1 :])

        *results, self.token = pl.pallas_call(
            kernel,
            out_shape=[*outs, jax.ShapeDtypeStruct((8, LANES), f32)],
            in_specs=in_specs + [free] * len(chained),
            out_specs=out_specs + [free],
            scratch_shapes=scratch,
            input_output_aliases=aliases,
            compiler_params=pltpu.CompilerParams(vmem_limit_bytes=vmem * MIB),
            cost_estimate=pl.CostEstimate(flops=0, bytes_accessed=0, transcendentals=0),
        )(*args, *chained)
        return results


def bf16_like(*shape):
    return jax.ShapeDtypeStruct(shape, bf16)


def f32_like(*shape):
    return jax.ShapeDtypeStruct(shape, f32)


def as_column(row):
    size = row.shape[1]
    diagonal = lax.broadcasted_iota(jnp.int32, (size, size), 0) == lax.broadcasted_iota(
        jnp.int32, (size, size), 1
    )
    return jnp.sum(jnp.where(diagonal, row, 0.0), axis=1, keepdims=True)


def as_row(column):
    size = column.shape[0]
    diagonal = lax.broadcasted_iota(jnp.int32, (size, size), 0) == lax.broadcasted_iota(
        jnp.int32, (size, size), 1
    )
    return jnp.sum(jnp.where(diagonal, column, 0.0), axis=0, keepdims=True)


def slot_rows(routing, experts, capacity):
    picks, tokens = routing.shape
    line = lax.broadcasted_iota(jnp.int32, (experts, tokens), 0)
    onehots = [(routing[k : k + 1] == line).astype(f32) for k in range(picks)]
    counted = functools.reduce(jnp.add, onehots)
    earlier = lax.broadcasted_iota(jnp.int32, (tokens, tokens), 0) < lax.broadcasted_iota(
        jnp.int32, (tokens, tokens), 1
    )
    before = jnp.dot(counted.astype(bf16), earlier.astype(bf16), preferred_element_type=f32)
    return [
        routing[k : k + 1].astype(f32) * capacity + jnp.sum(before * onehots[k], axis=0, keepdims=True)
        for k in range(picks)
    ]


def rows_for(first, count, slots, gates, dout):
    tokens = dout.shape[0]
    here = lax.broadcasted_iota(jnp.int32, (count, tokens), 0).astype(f32) + first
    hits = [here == row for row in slots]
    chosen = functools.reduce(jnp.logical_or, hits).astype(bf16)
    gate = functools.reduce(
        jnp.add, [jnp.sum(jnp.where(h, g, 0.0), axis=1, keepdims=True) for h, g in zip(hits, gates)]
    )
    return (jnp.dot(chosen, dout, preferred_element_type=f32) * gate).astype(bf16)


def pick_rows(first, slots_column, rows):
    lane = lax.broadcasted_iota(jnp.int32, (slots_column.shape[0], rows.shape[0]), 1).astype(f32)
    return jnp.dot((lane == slots_column - first).astype(bf16), rows, preferred_element_type=f32)


def start_body(capacity, routing_at, gates_at, dout_at, hidden_at, weight_at, *refs):
    message_ref, give_refs = refs[0], refs[1:5]
    routing_ref, gates_ref, dout_ref, hidden_ref, weight_ref, sems = refs[5:]
    units = weight_ref.shape[0]
    deep = units // WEIGHT_PARTS
    parts = [slice(at, at + deep) for at in range(0, units, deep)]
    moves = [
        pltpu.make_async_copy(a, b, sems.at[i])
        for i, (a, b) in enumerate(
            (
                (routing_at, routing_ref),
                (gates_at, gates_ref),
                (dout_at, dout_ref),
                (hidden_at, hidden_ref),
                *((weight_at.at[part], weight_ref.at[part]) for part in parts),
            )
        )
    ]
    for move in moves:
        move.start()
    me = lax.axis_index("expert")
    c = capacity
    picks, tokens = routing_ref.shape
    for move in moves[:3]:
        move.wait()
    routing = routing_ref[...]
    slots = slot_rows(routing, LINE, c)
    gates = [gates_ref[k : k + 1] for k in range(picks)]
    dout = dout_ref[...]
    lines = []
    for k in range(picks):
        expert = routing[k : k + 1].astype(f32)
        lines += [expert, slots[k] - expert * c]
        left = gates[k]
        for _ in range(PIECES):
            piece = left.astype(bf16).astype(f32)
            lines.append(piece)
            left = left - piece
    lines.append(jnp.zeros((LANES - len(lines), tokens), f32))
    width = dout.shape[1]
    message_ref[:, :width] = dout
    message_ref[:, width:] = jnp.concatenate(lines, axis=0).T.astype(bf16)
    for m, ref in enumerate(give_refs):
        first = ((me ^ m) * c).astype(f32)
        ref[:c] = rows_for(first, c, slots, gates, dout)
    moves[3].wait()
    rows = jnp.concatenate([hidden_ref[me ^ m] for m in range(4, LINE)], axis=0)
    total = None
    for part, move in zip(parts, moves[4:]):
        move.wait()
        product = jnp.dot(rows[:, part], weight_ref[part], preferred_element_type=f32)
        total = product if total is None else total + product
    out = total.astype(bf16)
    for m, ref in enumerate(give_refs):
        ref[c:] = out[m * c : (m + 1) * c]


def rest_body(hidden_ref, weight_ref, *refs):
    *out_refs, hidden_copy = refs
    me = lax.axis_index("expert")
    rows = jnp.concatenate([hidden_ref[me ^ m] for m in (0, 1, 3, 2)], axis=0)
    out = jnp.dot(rows, weight_ref[...], preferred_element_type=f32).astype(bf16)
    at = 0
    for ref in out_refs:
        ref[...] = out[at : at + ref.shape[0]]
        at += ref.shape[0]
    hidden_copy[...] = hidden_ref[...]


def message_lines(message_ref, picks):
    width = message_ref.shape[1] - LANES
    lines = message_ref[:, width:].astype(f32).T
    experts, ranks, gates = [], [], []
    for k in range(picks):
        at = k * (2 + PIECES)
        experts.append(lines[at : at + 1])
        ranks.append(lines[at + 1 : at + 2])
        gates.append(jnp.sum(lines[at + 2 : at + 2 + PIECES], axis=0, keepdims=True))
    return experts, ranks, gates, message_ref[:, :width]


def read_message(message_ref, picks, capacity):
    experts, ranks, gates, dout = message_lines(message_ref, picks)
    return [e * capacity + r for e, r in zip(experts, ranks)], gates, dout


def relay_body(capacity, picks, message_ref, *out_refs):
    me = lax.axis_index("expert")
    slots, gates, dout = read_message(message_ref, picks, capacity)
    m = 0
    for ref in out_refs:
        for at in range(0, ref.shape[0], capacity):
            first = ((me ^ m) * capacity).astype(f32)
            ref[at : at + capacity] = rows_for(first, capacity, slots, gates, dout)
            m += 1


def rows_to_hidden(rows, weight_ref, grad_part):
    grad = lax.dot_general(
        rows, weight_ref[...], (((1,), (1,)), ((), ())), preferred_element_type=f32
    ).astype(bf16)
    capacity = grad_part[0][0].shape[1]
    for at, (ref, block) in enumerate(grad_part):
        ref[block] = grad[at * capacity : (at + 1) * capacity]


def cut_slices(rows, slice_refs):
    group = lax.axis_index("dp")
    width = slice_refs[0].shape[1]
    for d, part in enumerate(slice_refs):
        part[...] = rows[:, pl.ds(pl.multiple_of((group ^ d) * width, width), width)]


def near_body(capacity, weight_ref, *refs):
    block_refs, grad_ref, slice_refs, rows = refs[:-6], refs[-6], refs[-5:-1], refs[-1]
    gather_blocks(capacity, block_refs, rows)
    rows_to_hidden(rows[...], weight_ref, [(grad_ref, m) for m in range(4)])
    cut_slices(rows, slice_refs)


def gather_blocks(capacity, refs, rows, start=0):
    for at, ref in enumerate(refs):
        rows[at * capacity : (at + 1) * capacity] = ref[start : start + capacity]


def far_body(capacity, weight_ref, near_grad_ref, *refs):
    block_refs, grad_ref, slice_refs, rows = refs[:-6], refs[-6], refs[-5:-1], refs[-1]
    me = lax.axis_index("expert")
    gather_blocks(capacity, block_refs, rows)
    for m in range(4):
        grad_ref[me ^ m] = near_grad_ref[m]
    rows_to_hidden(rows[...], weight_ref, [(grad_ref, me ^ m) for m in range(4, LINE)])
    cut_slices(rows, slice_refs)


def pack_body(*refs):
    hidden_refs, (near_ref, far_ref) = refs[:SQUARE], refs[-2:]
    me = lax.axis_index("expert")
    for ref, first in ((near_ref, 0), (far_ref, 4)):
        rows = jnp.concatenate([h[me ^ (first + m)] for h in hidden_refs for m in range(4)], axis=0)
        ref[...] = rows.T


def weight_body(columns_ref, *refs):
    slice_refs, others, out_ref = refs[:SQUARE], refs[SQUARE : SQUARE + 1], refs[-1]
    rows = jnp.concatenate([s[...] for s in slice_refs], axis=0)
    total = jnp.dot(columns_ref[...], rows, preferred_element_type=f32)
    for other in others if len(refs) > SQUARE + 1 else ():
        total = total + other[...]
    out_ref[...] = total


def share_body(capacity, own_ref, pair_ref, out_ref):
    out_ref[:capacity] = own_ref[...]
    out_ref[capacity:] = pair_ref[capacity:]


def blend(capacity, experts, ranks, gates, dout, rows):
    me = lax.axis_index("expert")
    dout = dout.astype(f32)
    total, products = 0.0, []
    for expert, rank, gate in zip(experts, ranks, gates):
        block = (expert.astype(jnp.int32) ^ me).astype(f32)
        picked = pick_rows(0.0, as_column(block * capacity + rank), rows)
        total += as_column(gate) * picked
        products.append(jnp.sum(picked * dout, axis=1, keepdims=True))
    return total, products


def blend_body(capacity, picks, message_ref, *refs):
    *block_refs, out_ref, rows = refs
    gather_blocks(capacity, block_refs, rows, capacity)
    experts, ranks, gates, dout = message_lines(message_ref, picks)
    total, products = blend(capacity, experts, ranks, gates, dout, rows[...])
    width = dout.shape[1]
    out_ref[:, :width] = total.astype(bf16)
    lane = lax.broadcasted_iota(jnp.int32, (total.shape[0], LANES), 1)
    beside = jnp.zeros(lane.shape, f32)
    at = 0
    for left in products:
        for _ in range(PIECES):
            piece = left.astype(bf16).astype(f32)
            beside = jnp.where(lane == at, piece, beside)
            left = left - piece
            at += 1
    out_ref[:, width:] = beside.astype(bf16)


def combine_body(capacity, message_ref, own_ref, pair_ref, hop_ref, far_ref, *refs):
    combined_ref, grad_gates_ref, rows = refs
    c = capacity
    picks = grad_gates_ref.shape[0]
    rows[:c] = own_ref[...]
    rows[c : 2 * c] = pair_ref[:c]
    rows[2 * c :] = hop_ref[...]
    experts, ranks, gates, dout = message_lines(message_ref, picks)
    total, products = blend(c, experts, ranks, gates, dout, rows[...])
    width = dout.shape[1]
    combined_ref[...] = (total + far_ref[:, :width].astype(f32)).astype(bf16)
    beside = far_ref[:, width:].astype(f32)
    for k, near in enumerate(products):
        far = jnp.sum(beside[:, k * PIECES : (k + 1) * PIECES], axis=1, keepdims=True)
        grad_gates_ref[k : k + 1] = as_row(near + far)


class Plan:
    def __init__(self, **values):
        self.values = values
        self.moves = {}
        self.run = Steps()

    def move(self, name, source, axis, m):
        self.moves[name] = (source, axis, m)

    def value(self, name):
        if name not in self.values:
            source, axis, m = self.moves[name]
            size = lax.axis_size(axis)
            self.values[name] = lax.ppermute(
                self.value(source), axis, [(i, i ^ m) for i in range(size)]
            )
        return self.values[name]

    def step(self, body, outs, ins, waits=(), held=(), **options):
        n, w, h, o = len(ins), len(waits), len(held), len(outs)
        args = [self.value(name) for name in (*ins, *waits, *held)]

        def whole(*refs):
            rest = refs[n + w + h :]
            body(*refs[:n], *rest[:o], *rest[o + h :])

        results = self.run(
            whole,
            [*outs.values(), *(jax.ShapeDtypeStruct(a.shape, a.dtype) for a in args[n + w :])],
            args,
            anywhere=tuple(range(n, n + w)),
            aliases={n + w + k: o + k for k in range(h)},
            **options,
        )
        self.values.update(zip((*outs, *held), results))


def on_device(routing, gates, hidden, w_down, dout):
    capacity, units = hidden.shape[3:]
    width = w_down.shape[2]
    tokens, picks = routing.shape
    part = width // SQUARE
    plan = Plan(
        routing=routing.T, gates=gates.T, hidden=hidden[0, 0], weight=w_down[0], dout=dout
    )
    step, move = plan.step, plan.move

    def block(count):
        return bf16_like(count * capacity, width)

    slices = bf16_like(4 * capacity, part)
    rows_scratch = [pltpu.VMEM((4 * capacity, width), bf16)]

    move("peer1", "hidden_copy", "dp", 1)
    move("peer2", "hidden_copy", "dp", 2)
    move("peer3", "peer1", "dp", 2)
    move("from_afar", "message", "expert", 4)
    for m in (1, 2, 3):
        move(f"near{m}", f"give{m}", "expert", m)
        move(f"far{m}", f"relay{m}", "expert", m)
        move(f"near_slice{m}", f"near_cut{m}", "dp", m)
        move(f"far_slice{m}", f"far_cut{m}", "dp", m)
    move("pair_near", "rows_near", "expert", 1)
    move("hop_near", "share_near", "expert", 2)
    move("blended", "blend", "expert", 4)

    step(
        functools.partial(start_body, capacity),
        dict(
            message=bf16_like(tokens, width + LANES),
            **{f"give{m}": block(2) for m in range(4)},
        ),
        ["routing", "gates", "dout", "hidden", "weight"],
        scratch=[
            pltpu.VMEM((picks, tokens), jnp.int32),
            pltpu.VMEM((picks, tokens), f32),
            pltpu.VMEM((tokens, width), bf16),
            pltpu.VMEM((LINE, capacity, units), bf16),
            pltpu.VMEM((units, width), bf16),
            pltpu.SemaphoreType.DMA((4 + WEIGHT_PARTS,)),
        ],
        pinned=(0, 1, 2, 3, 4),
        vmem=VMEM_ALL,
    )

    def rest(**o):
        step(
            rest_body,
            dict(
                rows0=block(1),
                rows_near=block(2),
                rows2=block(1),
                hidden_copy=bf16_like(LINE, capacity, units),
            ),
            ["hidden", "weight"],
            **o,
        )

    def near(**o):
        step(
            functools.partial(near_body, capacity),
            dict(near_grad=bf16_like(4, capacity, units), **{f"near_cut{d}": slices for d in range(SQUARE)}),
            ["weight", "give0", "near1", "near2", "near3"],
            scratch=rows_scratch,
            **o,
        )

    def relay(**o):
        step(
            functools.partial(relay_body, capacity, picks),
            {f"relay{m}": block(1) for m in range(4)},
            ["from_afar"],
            **o,
        )

    def pack(**o):
        step(
            pack_body,
            dict(near_columns=bf16_like(units, SQUARE * 4 * capacity), far_columns=bf16_like(units, SQUARE * 4 * capacity)),
            ["hidden", "peer1", "peer2", "peer3"],
            **o,
        )

    def near_weight(**o):
        step(
            weight_body,
            dict(near_weight=f32_like(units, part)),
            ["near_columns", "near_cut0", "near_slice1", "near_slice2", "near_slice3"],
            **o,
        )

    def far(**o):
        step(
            functools.partial(far_body, capacity),
            dict(grad_hidden=bf16_like(LINE, capacity, units), **{f"far_cut{d}": slices for d in range(SQUARE)}),
            ["weight", "near_grad", "relay0", "far1", "far2", "far3"],
            scratch=rows_scratch,
            **o,
        )

    def far_weight(**o):
        step(
            weight_body,
            dict(grad_down=f32_like(units, part)),
            ["far_columns", "far_cut0", "far_slice1", "far_slice2", "far_slice3", "near_weight"],
            **o,
        )

    def share(name, own, **o):
        step(
            functools.partial(share_body, capacity),
            {f"share_{name}": block(2)},
            [own, f"pair_{name}"],
            **o,
        )

    def gate(*waits, held=()):
        step(lambda *_: None, {}, [], waits=waits, held=held)

    def blend(**o):
        step(
            functools.partial(blend_body, capacity, picks),
            dict(blend=bf16_like(tokens, width + LANES)),
            ["from_afar", "give0", "near1", "near2", "near3"],
            scratch=rows_scratch,
            **o,
        )

    def combine(**o):
        step(
            functools.partial(combine_body, capacity),
            dict(combined=bf16_like(tokens, width), grad_gates=f32_like(picks, tokens)),
            ["message", "rows0", "pair_near", "hop_near", "blended"],
            scratch=rows_scratch,
            **o,
        )

    rest(waits=["near1"])
    relay(waits=["peer1", "peer2"])
    near()
    blend()
    share("near", "rows2")
    far()
    pack()
    near_weight()
    far_weight()
    combine()
    v = plan.values
    return (v["combined"], v["grad_gates"].T, v["grad_hidden"][None, None], v["grad_down"][None])


def slot_index(routing, experts, capacity):
    flattened = routing.reshape(-1)
    onehot = (flattened[:, None] == jnp.arange(experts, dtype=jnp.int32)[None, :]).astype(jnp.int32)
    before = jnp.cumsum(onehot, axis=0) - onehot
    ranking = jnp.sum(before * onehot, axis=1)
    return flattened * capacity + ranking


def on_device_any(routing, gates, hidden, w_down, dout):
    experts = lax.axis_size("expert")
    capacity = hidden.shape[3]
    hidden_units = w_down.shape[1]
    model_width = w_down.shape[2]
    tok_rows = routing.shape[0]
    picks_per = routing.shape[1]
    weight = w_down[0]
    input_rows = hidden[0, 0].reshape(-1, hidden_units)
    outputs = jnp.dot(input_rows, weight, preferred_element_type=jnp.float32).astype(jnp.bfloat16)
    outputs = outputs.reshape(experts, capacity, model_width)
    returned = lax.all_to_all(outputs, "expert", split_axis=0, concat_axis=0, tiled=True)
    location = slot_index(routing, experts, capacity)
    picked = jnp.take(returned.reshape(experts * capacity, model_width), location, axis=0)
    picked = picked.reshape(tok_rows, picks_per, model_width).astype(jnp.float32)
    combined = jnp.sum(gates[..., None] * picked, axis=1).astype(jnp.bfloat16)
    grad_float = dout.astype(jnp.float32)
    grad_gates = jnp.sum(picked * grad_float[:, None, :], axis=2)
    scaled = (
        (gates[..., None] * grad_float[:, None, :]).astype(jnp.bfloat16).reshape(-1, model_width)
    )
    slot_grads = jnp.zeros((experts * capacity, model_width), jnp.bfloat16).at[location].set(scaled)
    slot_grads = slot_grads.reshape(experts, capacity, model_width)
    received = lax.all_to_all(slot_grads, "expert", split_axis=0, concat_axis=0, tiled=True)
    count_items = received.shape[1]
    flattened = received.reshape(-1, model_width)
    grad_rows = lax.dot_general(
        flattened, weight, (((1,), (1,)), ((), ())), preferred_element_type=jnp.float32
    )
    grad_hidden = grad_rows.astype(jnp.bfloat16).reshape(experts, count_items, hidden_units)
    arrived_rows = received.reshape(-1, model_width)
    partial_grad = lax.dot_general(
        input_rows, arrived_rows, (((0,), (0,)), ((), ())), preferred_element_type=jnp.float32
    )
    grad_down = lax.psum_scatter(
        partial_grad.astype(jnp.bfloat16), "dp", scatter_dimension=1, tiled=True
    ).astype(jnp.float32)
    return (combined, grad_gates, grad_hidden[None, None], grad_down[None])


def solution(mesh):
    placed = (
        P(("dp", "expert"), None),
        P(("dp", "expert"), None),
        P("dp", "expert", None, None, None),
        P("expert", None, None),
        P(("dp", "expert"), None),
    )
    planned = mesh.shape["expert"] == LINE and mesh.shape["dp"] == SQUARE
    return jax.shard_map(
        on_device if planned else on_device_any,
        mesh=mesh,
        in_specs=placed,
        out_specs=(
            P(("dp", "expert"), None),
            P(("dp", "expert"), None),
            P("dp", "expert", None, None, None),
            P("expert", None, "dp"),
        ),
        check_vma=False,
    )
```

```python
import functools

import jax
import jax.numpy as jnp
from jax import lax
from jax.experimental import pallas as pl
from jax.experimental.pallas import tpu as pltpu
from jax.sharding import PartitionSpec as P

LINE = 8
SQUARE = 4
LANES = 128
WEIGHT_PARTS = 3
PIECES = 3
MIB = 1 << 20
VMEM_ALL = 60
f32, bf16 = jnp.float32, jnp.bfloat16


class Steps:
    def __init__(self):
        self.token = None

    def __call__(self, body, outs, args, scratch=(), vmem=40, aliases=None, anywhere=(), pinned=()):
        aliases = aliases or {}
        whole = pl.BlockSpec(memory_space=pltpu.VMEM)
        free = pl.BlockSpec(memory_space=pl.ANY)
        fixed = pl.BlockSpec(memory_space=pltpu.HBM)
        in_specs = [
            fixed if i in pinned else free if i in aliases or i in anywhere else whole
            for i in range(len(args))
        ]
        out_specs = [free if o in aliases.values() else whole for o in range(len(outs))]
        n_args, n_outs = len(args), len(outs)
        chained = () if self.token is None else (self.token,)

        def kernel(*refs):
            rest = refs[n_args + len(chained) :]
            body(*refs[:n_args], *rest[:n_outs], *rest[n_outs + 1 :])

        *results, self.token = pl.pallas_call(
            kernel,
            out_shape=[*outs, jax.ShapeDtypeStruct((8, LANES), f32)],
            in_specs=in_specs + [free] * len(chained),
            out_specs=out_specs + [free],
            scratch_shapes=scratch,
            input_output_aliases=aliases,
            compiler_params=pltpu.CompilerParams(vmem_limit_bytes=vmem * MIB),
            cost_estimate=pl.CostEstimate(flops=0, bytes_accessed=0, transcendentals=0),
        )(*args, *chained)
        return results


def bf16_like(*shape):
    return jax.ShapeDtypeStruct(shape, bf16)


def f32_like(*shape):
    return jax.ShapeDtypeStruct(shape, f32)


def as_column(row):
    size = row.shape[1]
    diagonal = lax.broadcasted_iota(jnp.int32, (size, size), 0) == lax.broadcasted_iota(
        jnp.int32, (size, size), 1
    )
    return jnp.sum(jnp.where(diagonal, row, 0.0), axis=1, keepdims=True)


def as_row(column):
    size = column.shape[0]
    diagonal = lax.broadcasted_iota(jnp.int32, (size, size), 0) == lax.broadcasted_iota(
        jnp.int32, (size, size), 1
    )
    return jnp.sum(jnp.where(diagonal, column, 0.0), axis=0, keepdims=True)


def slot_rows(routing, experts, capacity):
    picks, tokens = routing.shape
    line = lax.broadcasted_iota(jnp.int32, (experts, tokens), 0)
    onehots = [(routing[k : k + 1] == line).astype(f32) for k in range(picks)]
    counted = functools.reduce(jnp.add, onehots)
    earlier = lax.broadcasted_iota(jnp.int32, (tokens, tokens), 0) < lax.broadcasted_iota(
        jnp.int32, (tokens, tokens), 1
    )
    before = jnp.dot(counted.astype(bf16), earlier.astype(bf16), preferred_element_type=f32)
    return [
        routing[k : k + 1].astype(f32) * capacity + jnp.sum(before * onehots[k], axis=0, keepdims=True)
        for k in range(picks)
    ]


def rows_for(first, count, slots, gates, dout):
    tokens = dout.shape[0]
    here = lax.broadcasted_iota(jnp.int32, (count, tokens), 0).astype(f32) + first
    hits = [here == row for row in slots]
    chosen = functools.reduce(jnp.logical_or, hits).astype(bf16)
    gate = functools.reduce(
        jnp.add, [jnp.sum(jnp.where(h, g, 0.0), axis=1, keepdims=True) for h, g in zip(hits, gates)]
    )
    return (jnp.dot(chosen, dout, preferred_element_type=f32) * gate).astype(bf16)


def pick_rows(first, slots_column, rows):
    lane = lax.broadcasted_iota(jnp.int32, (slots_column.shape[0], rows.shape[0]), 1).astype(f32)
    return jnp.dot((lane == slots_column - first).astype(bf16), rows, preferred_element_type=f32)


def start_body(capacity, routing_at, gates_at, dout_at, hidden_at, weight_at, *refs):
    message_ref, give_refs = refs[0], refs[1:5]
    routing_ref, gates_ref, dout_ref, hidden_ref, weight_ref, sems = refs[5:]
    me = lax.axis_index("expert")
    units = weight_ref.shape[0]
    deep = units // WEIGHT_PARTS
    parts = [slice(at, at + deep) for at in range(0, units, deep)]
    moves = [
        pltpu.make_async_copy(a, b, sems.at[i])
        for i, (a, b) in enumerate(
            (
                (routing_at, routing_ref),
                (gates_at, gates_ref),
                (dout_at, dout_ref),
                *((hidden_at.at[me ^ (4 + m)], hidden_ref.at[m]) for m in range(4)),
                *((weight_at.at[part], weight_ref.at[part]) for part in parts),
            )
        )
    ]
    for move in moves:
        move.start()
    c = capacity
    picks, tokens = routing_ref.shape
    for move in moves[:3]:
        move.wait()
    routing = routing_ref[...]
    slots = slot_rows(routing, LINE, c)
    gates = [gates_ref[k : k + 1] for k in range(picks)]
    dout = dout_ref[...]
    lines = []
    for k in range(picks):
        expert = routing[k : k + 1].astype(f32)
        lines += [expert, slots[k] - expert * c]
        left = gates[k]
        for _ in range(PIECES):
            piece = left.astype(bf16).astype(f32)
            lines.append(piece)
            left = left - piece
    lines.append(jnp.zeros((LANES - len(lines), tokens), f32))
    width = dout.shape[1]
    message_ref[:, :width] = dout
    message_ref[:, width:] = jnp.concatenate(lines, axis=0).T.astype(bf16)
    for m, ref in enumerate(give_refs):
        first = ((me ^ m) * c).astype(f32)
        ref[:c] = rows_for(first, c, slots, gates, dout)
    for move in moves[3:7]:
        move.wait()
    rows = jnp.concatenate([hidden_ref[m] for m in range(4)], axis=0)
    total = None
    for part, move in zip(parts, moves[7:]):
        move.wait()
        product = jnp.dot(rows[:, part], weight_ref[part], preferred_element_type=f32)
        total = product if total is None else total + product
    out = total.astype(bf16)
    for m, ref in enumerate(give_refs):
        ref[c:] = out[m * c : (m + 1) * c]


def rest_body(hidden_ref, weight_ref, *refs):
    *out_refs, hidden_copy = refs
    me = lax.axis_index("expert")
    rows = jnp.concatenate([hidden_ref[me ^ m] for m in (0, 1, 3, 2)], axis=0)
    out = jnp.dot(rows, weight_ref[...], preferred_element_type=f32).astype(bf16)
    at = 0
    for ref in out_refs:
        ref[...] = out[at : at + ref.shape[0]]
        at += ref.shape[0]
    hidden_copy[...] = hidden_ref[...]


def message_lines(message_ref, picks):
    width = message_ref.shape[1] - LANES
    lines = message_ref[:, width:].astype(f32).T
    experts, ranks, gates = [], [], []
    for k in range(picks):
        at = k * (2 + PIECES)
        experts.append(lines[at : at + 1])
        ranks.append(lines[at + 1 : at + 2])
        gates.append(jnp.sum(lines[at + 2 : at + 2 + PIECES], axis=0, keepdims=True))
    return experts, ranks, gates, message_ref[:, :width]


def read_message(message_ref, picks, capacity):
    experts, ranks, gates, dout = message_lines(message_ref, picks)
    return [e * capacity + r for e, r in zip(experts, ranks)], gates, dout


def relay_body(capacity, picks, message_ref, *out_refs):
    me = lax.axis_index("expert")
    slots, gates, dout = read_message(message_ref, picks, capacity)
    m = 0
    for ref in out_refs:
        for at in range(0, ref.shape[0], capacity):
            first = ((me ^ m) * capacity).astype(f32)
            ref[at : at + capacity] = rows_for(first, capacity, slots, gates, dout)
            m += 1


def rows_to_hidden(rows, weight_ref, grad_part):
    grad = lax.dot_general(
        rows, weight_ref[...], (((1,), (1,)), ((), ())), preferred_element_type=f32
    ).astype(bf16)
    capacity = grad_part[0][0].shape[1]
    for at, (ref, block) in enumerate(grad_part):
        ref[block] = grad[at * capacity : (at + 1) * capacity]


def cut_slices(rows, slice_refs):
    group = lax.axis_index("dp")
    width = slice_refs[0].shape[1]
    for d, part in enumerate(slice_refs):
        part[...] = rows[:, pl.ds(pl.multiple_of((group ^ d) * width, width), width)]


def near_body(capacity, weight_ref, *refs):
    block_refs, grad_ref, slice_refs, rows = refs[:-6], refs[-6], refs[-5:-1], refs[-1]
    gather_blocks(capacity, block_refs, rows)
    rows_to_hidden(rows[...], weight_ref, [(grad_ref, m) for m in range(4)])
    cut_slices(rows, slice_refs)


def gather_blocks(capacity, refs, rows, start=0):
    for at, ref in enumerate(refs):
        rows[at * capacity : (at + 1) * capacity] = ref[start : start + capacity]


def far_body(capacity, weight_ref, near_grad_ref, *refs):
    block_refs, grad_ref, slice_refs, rows = refs[:-6], refs[-6], refs[-5:-1], refs[-1]
    me = lax.axis_index("expert")
    gather_blocks(capacity, block_refs, rows)
    for m in range(4):
        grad_ref[me ^ m] = near_grad_ref[m]
    rows_to_hidden(rows[...], weight_ref, [(grad_ref, me ^ m) for m in range(4, LINE)])
    cut_slices(rows, slice_refs)


def pack_body(*refs):
    hidden_refs, (near_ref, far_ref) = refs[:SQUARE], refs[-2:]
    me = lax.axis_index("expert")
    for ref, first in ((near_ref, 0), (far_ref, 4)):
        rows = jnp.concatenate([h[me ^ (first + m)] for h in hidden_refs for m in range(4)], axis=0)
        ref[...] = rows.T


def weight_body(columns_ref, *refs):
    slice_refs, others, out_ref = refs[:SQUARE], refs[SQUARE : SQUARE + 1], refs[-1]
    rows = jnp.concatenate([s[...] for s in slice_refs], axis=0)
    total = jnp.dot(columns_ref[...], rows, preferred_element_type=f32)
    for other in others if len(refs) > SQUARE + 1 else ():
        total = total + other[...]
    out_ref[...] = total


def share_body(capacity, own_ref, pair_ref, out_ref):
    out_ref[:capacity] = own_ref[...]
    out_ref[capacity:] = pair_ref[capacity:]


def blend(capacity, experts, ranks, gates, dout, rows):
    me = lax.axis_index("expert")
    dout = dout.astype(f32)
    total, products = 0.0, []
    for expert, rank, gate in zip(experts, ranks, gates):
        block = (expert.astype(jnp.int32) ^ me).astype(f32)
        picked = pick_rows(0.0, as_column(block * capacity + rank), rows)
        total += as_column(gate) * picked
        products.append(jnp.sum(picked * dout, axis=1, keepdims=True))
    return total, products


def blend_body(capacity, picks, message_ref, *refs):
    *block_refs, out_ref, rows = refs
    gather_blocks(capacity, block_refs, rows, capacity)
    experts, ranks, gates, dout = message_lines(message_ref, picks)
    total, products = blend(capacity, experts, ranks, gates, dout, rows[...])
    width = dout.shape[1]
    out_ref[:, :width] = total.astype(bf16)
    lane = lax.broadcasted_iota(jnp.int32, (total.shape[0], LANES), 1)
    beside = jnp.zeros(lane.shape, f32)
    at = 0
    for left in products:
        for _ in range(PIECES):
            piece = left.astype(bf16).astype(f32)
            beside = jnp.where(lane == at, piece, beside)
            left = left - piece
            at += 1
    out_ref[:, width:] = beside.astype(bf16)


def combine_body(capacity, message_ref, own_ref, pair_ref, hop_ref, far_ref, *refs):
    combined_ref, grad_gates_ref, rows = refs
    c = capacity
    picks = grad_gates_ref.shape[0]
    rows[:c] = own_ref[...]
    rows[c : 2 * c] = pair_ref[:c]
    rows[2 * c :] = hop_ref[...]
    experts, ranks, gates, dout = message_lines(message_ref, picks)
    total, products = blend(c, experts, ranks, gates, dout, rows[...])
    width = dout.shape[1]
    combined_ref[...] = (total + far_ref[:, :width].astype(f32)).astype(bf16)
    beside = far_ref[:, width:].astype(f32)
    for k, near in enumerate(products):
        far = jnp.sum(beside[:, k * PIECES : (k + 1) * PIECES], axis=1, keepdims=True)
        grad_gates_ref[k : k + 1] = as_row(near + far)


class Plan:
    def __init__(self, **values):
        self.values = values
        self.moves = {}
        self.run = Steps()

    def move(self, name, source, axis, m):
        self.moves[name] = (source, axis, m)

    def value(self, name):
        if name not in self.values:
            source, axis, m = self.moves[name]
            size = lax.axis_size(axis)
            self.values[name] = lax.ppermute(
                self.value(source), axis, [(i, i ^ m) for i in range(size)]
            )
        return self.values[name]

    def step(self, body, outs, ins, waits=(), held=(), **options):
        n, w, h, o = len(ins), len(waits), len(held), len(outs)
        args = [self.value(name) for name in (*ins, *waits, *held)]

        def whole(*refs):
            rest = refs[n + w + h :]
            body(*refs[:n], *rest[:o], *rest[o + h :])

        results = self.run(
            whole,
            [*outs.values(), *(jax.ShapeDtypeStruct(a.shape, a.dtype) for a in args[n + w :])],
            args,
            anywhere=tuple(range(n, n + w)),
            aliases={n + w + k: o + k for k in range(h)},
            **options,
        )
        self.values.update(zip((*outs, *held), results))


def on_device(routing, gates, hidden, w_down, dout):
    capacity, units = hidden.shape[3:]
    width = w_down.shape[2]
    tokens, picks = routing.shape
    part = width // SQUARE
    plan = Plan(
        routing=routing.T, gates=gates.T, hidden=hidden[0, 0], weight=w_down[0], dout=dout
    )
    step, move = plan.step, plan.move

    def block(count):
        return bf16_like(count * capacity, width)

    slices = bf16_like(4 * capacity, part)
    rows_scratch = [pltpu.VMEM((4 * capacity, width), bf16)]

    move("peer1", "hidden_copy", "dp", 1)
    move("peer2", "hidden_copy", "dp", 2)
    move("peer3", "peer1", "dp", 2)
    move("from_afar", "message", "expert", 4)
    for m in (1, 2, 3):
        move(f"near{m}", f"give{m}", "expert", m)
        move(f"far{m}", f"relay{m}", "expert", m)
        move(f"near_slice{m}", f"near_cut{m}", "dp", m)
        move(f"far_slice{m}", f"far_cut{m}", "dp", m)
    move("pair_near", "rows_near", "expert", 1)
    move("hop_near", "share_near", "expert", 2)
    move("blended", "blend", "expert", 4)

    step(
        functools.partial(start_body, capacity),
        dict(
            message=bf16_like(tokens, width + LANES),
            **{f"give{m}": block(2) for m in range(4)},
        ),
        ["routing", "gates", "dout", "hidden", "weight"],
        scratch=[
            pltpu.VMEM((picks, tokens), jnp.int32),
            pltpu.VMEM((picks, tokens), f32),
            pltpu.VMEM((tokens, width), bf16),
            pltpu.VMEM((4, capacity, units), bf16),
            pltpu.VMEM((units, width), bf16),
            pltpu.SemaphoreType.DMA((7 + WEIGHT_PARTS,)),
        ],
        pinned=(0, 1, 2, 3, 4),
        vmem=VMEM_ALL,
    )

    def rest(**o):
        step(
            rest_body,
            dict(
                rows0=block(1),
                rows_near=block(2),
                rows2=block(1),
                hidden_copy=bf16_like(LINE, capacity, units),
            ),
            ["hidden", "weight"],
            **o,
        )

    def near(**o):
        step(
            functools.partial(near_body, capacity),
            dict(near_grad=bf16_like(4, capacity, units), **{f"near_cut{d}": slices for d in range(SQUARE)}),
            ["weight", "give0", "near1", "near2", "near3"],
            scratch=rows_scratch,
            **o,
        )

    def relay(**o):
        step(
            functools.partial(relay_body, capacity, picks),
            {f"relay{m}": block(1) for m in range(4)},
            ["from_afar"],
            **o,
        )

    def pack(**o):
        step(
            pack_body,
            dict(near_columns=bf16_like(units, SQUARE * 4 * capacity), far_columns=bf16_like(units, SQUARE * 4 * capacity)),
            ["hidden", "peer1", "peer2", "peer3"],
            **o,
        )

    def near_weight(**o):
        step(
            weight_body,
            dict(near_weight=f32_like(units, part)),
            ["near_columns", "near_cut0", "near_slice1", "near_slice2", "near_slice3"],
            **o,
        )

    def far(**o):
        step(
            functools.partial(far_body, capacity),
            dict(grad_hidden=bf16_like(LINE, capacity, units), **{f"far_cut{d}": slices for d in range(SQUARE)}),
            ["weight", "near_grad", "relay0", "far1", "far2", "far3"],
            scratch=rows_scratch,
            **o,
        )

    def far_weight(**o):
        step(
            weight_body,
            dict(grad_down=f32_like(units, part)),
            ["far_columns", "far_cut0", "far_slice1", "far_slice2", "far_slice3", "near_weight"],
            **o,
        )

    def share(name, own, **o):
        step(
            functools.partial(share_body, capacity),
            {f"share_{name}": block(2)},
            [own, f"pair_{name}"],
            **o,
        )

    def gate(*waits, held=()):
        step(lambda *_: None, {}, [], waits=waits, held=held)

    def blend(**o):
        step(
            functools.partial(blend_body, capacity, picks),
            dict(blend=bf16_like(tokens, width + LANES)),
            ["from_afar", "give0", "near1", "near2", "near3"],
            scratch=rows_scratch,
            **o,
        )

    def combine(**o):
        step(
            functools.partial(combine_body, capacity),
            dict(combined=bf16_like(tokens, width), grad_gates=f32_like(picks, tokens)),
            ["message", "rows0", "pair_near", "hop_near", "blended"],
            scratch=rows_scratch,
            **o,
        )

    rest(waits=["near1"])
    relay(waits=["peer1", "peer2"])
    near()
    blend()
    share("near", "rows2")
    far()
    pack()
    near_weight()
    far_weight()
    combine()
    v = plan.values
    return (v["combined"], v["grad_gates"].T, v["grad_hidden"][None, None], v["grad_down"][None])


def slot_index(routing, experts, capacity):
    flattened = routing.reshape(-1)
    onehot = (flattened[:, None] == jnp.arange(experts, dtype=jnp.int32)[None, :]).astype(jnp.int32)
    before = jnp.cumsum(onehot, axis=0) - onehot
    ranking = jnp.sum(before * onehot, axis=1)
    return flattened * capacity + ranking


def on_device_any(routing, gates, hidden, w_down, dout):
    experts = lax.axis_size("expert")
    capacity = hidden.shape[3]
    hidden_units = w_down.shape[1]
    model_width = w_down.shape[2]
    tok_rows = routing.shape[0]
    picks_per = routing.shape[1]
    weight = w_down[0]
    input_rows = hidden[0, 0].reshape(-1, hidden_units)
    outputs = jnp.dot(input_rows, weight, preferred_element_type=jnp.float32).astype(jnp.bfloat16)
    outputs = outputs.reshape(experts, capacity, model_width)
    returned = lax.all_to_all(outputs, "expert", split_axis=0, concat_axis=0, tiled=True)
    location = slot_index(routing, experts, capacity)
    picked = jnp.take(returned.reshape(experts * capacity, model_width), location, axis=0)
    picked = picked.reshape(tok_rows, picks_per, model_width).astype(jnp.float32)
    combined = jnp.sum(gates[..., None] * picked, axis=1).astype(jnp.bfloat16)
    grad_float = dout.astype(jnp.float32)
    grad_gates = jnp.sum(picked * grad_float[:, None, :], axis=2)
    scaled = (
        (gates[..., None] * grad_float[:, None, :]).astype(jnp.bfloat16).reshape(-1, model_width)
    )
    slot_grads = jnp.zeros((experts * capacity, model_width), jnp.bfloat16).at[location].set(scaled)
    slot_grads = slot_grads.reshape(experts, capacity, model_width)
    received = lax.all_to_all(slot_grads, "expert", split_axis=0, concat_axis=0, tiled=True)
    count_items = received.shape[1]
    flattened = received.reshape(-1, model_width)
    grad_rows = lax.dot_general(
        flattened, weight, (((1,), (1,)), ((), ())), preferred_element_type=jnp.float32
    )
    grad_hidden = grad_rows.astype(jnp.bfloat16).reshape(experts, count_items, hidden_units)
    arrived_rows = received.reshape(-1, model_width)
    partial_grad = lax.dot_general(
        input_rows, arrived_rows, (((0,), (0,)), ((), ())), preferred_element_type=jnp.float32
    )
    grad_down = lax.psum_scatter(
        partial_grad.astype(jnp.bfloat16), "dp", scatter_dimension=1, tiled=True
    ).astype(jnp.float32)
    return (combined, grad_gates, grad_hidden[None, None], grad_down[None])


def solution(mesh):
    placed = (
        P(("dp", "expert"), None),
        P(("dp", "expert"), None),
        P("dp", "expert", None, None, None),
        P("expert", None, None),
        P(("dp", "expert"), None),
    )
    planned = mesh.shape["expert"] == LINE and mesh.shape["dp"] == SQUARE
    return jax.shard_map(
        on_device if planned else on_device_any,
        mesh=mesh,
        in_specs=placed,
        out_specs=(
            P(("dp", "expert"), None),
            P(("dp", "expert"), None),
            P("dp", "expert", None, None, None),
            P("expert", None, "dp"),
        ),
        check_vma=False,
    )
```
